512 devices in a mesh: dp: 4 (over x), tm: 128 (over y, z, core).
Axes of the slice: x: 4, y: 8, z: 8, core: 2. Of those that a mesh axis runs over, the one named last changes fastest.
Arguments:
- query_rows: bfloat16 [4, 16384, 512], P('dp', 'tm'), may hold values from -60 to 60
- key_rows: bfloat16 [4, 16384, 512], P('dp', 'tm'), may hold values from -4 to 4
- value_rows: bfloat16 [4, 16384, 512], P('dp', 'tm'), may hold values from -6 to 6
- out_grad: bfloat16 [4, 16384, 1024], P('dp', 'tm'), may hold values from -6 to 6
- out_weight: bfloat16 [512, 1024], replicated, may hold values from -0.25 to 0.25
- memory_index: int32 [4, 128, 8], P('dp', 'tm'), may hold values from 0 to 127, as said below
Outputs:
- query_grad: bfloat16 [4, 16384, 512], P('dp', 'tm')
- key_grad: bfloat16 [4, 16384, 512], P('dp', 'tm')
- value_grad: bfloat16 [4, 16384, 512], P('dp', 'tm')
- weight_grad: bfloat16 [512, 1024], replicated
The draws below stay inside these ranges and needn't reach their ends.
Inputs may be any that keep to these rules, and one draw needn't show every extreme that they name: `memory_index`: each row holds 8 distinct positions of its segment.
All inputs are finite; a program needn't handle non-finite values.
Results may differ from the reference program's by a relative error of at most 0.028.
Values may be sent and summed in bfloat16 or wider, within the bound.
A program may use at most 64 MiB of HBM per device.

```python
import math
import jax
import jax.numpy as jnp
from jax import lax

D = 1024
HEADS = 8
HEAD_DIM = 64
SEG = 128
MEM = 8
HD = 512
SEGS = 128
CLIPS = 4
TOKENS = 16384


def shared_rows(key):
    base = jax.random.uniform(key, (CLIPS, TOKENS, HD), jnp.float32, -1.7320508, 1.7320508)
    position = jnp.arange(TOKENS, dtype=jnp.int32) % 8
    copied = base
    return jnp.where((position == 6)[None, :, None], copied, base)


def draw_key_rows(key, part):
    return shared_rows(key).astype(jnp.bfloat16)


def draw_query_rows(key, part):
    key = jax.random.fold_in(key, 11)
    result = jax.random.truncated_normal(key, -4.0, 4.0, (CLIPS, TOKENS, HD), jnp.float32)
    return result.astype(jnp.bfloat16)


def draw_memory_index(key, part):
    key = jax.random.fold_in(key, 5)
    subkeys = jax.random.split(key, CLIPS * SEGS)

    def pick_row(subkey):
        return jax.random.permutation(subkey, SEG)[:MEM]
    picked = jax.vmap(pick_row)(subkeys)
    return picked.reshape(CLIPS, SEGS, MEM).astype(jnp.int32)


def steps_of(rng, extent, cuts, low, high):
    loudness, own = 1.0, jax.random.fold_in(rng, 6)
    for axis_at, parts in cuts:
        steps = jnp.exp(jax.random.uniform(jax.random.fold_in(own, axis_at), (parts,), jnp.float32, low / len(cuts), high / len(cuts)))
        loudness = loudness * jnp.repeat(steps, extent[axis_at] // parts).reshape([-1 if axis == axis_at else 1 for axis in range(len(extent))])
    return loudness


def noise(key, dims, spread, bound, cuts=(), held_as=jnp.bfloat16):
    values = jax.random.normal(key, dims, jnp.float32) * spread
    if len(cuts) > 0:
        values = steps_of(key, dims, cuts, -0.22, 0.18) * values
    return jnp.clip(values, min=-bound, max=bound).astype(held_as)


def setup_inputs(seed: int = 0) -> dict:
    keys = jax.random.split(jax.random.key(seed), 7)
    return {
        "query_rows": draw_query_rows(jax.random.fold_in(keys[6], 71), 0),
        "key_rows": draw_key_rows(jax.random.fold_in(keys[6], 71), 0),
        "value_rows": noise(keys[2], (CLIPS, TOKENS, HD), 1.0, 6.0, ((0, 4), (1, 128))),
        "out_grad": noise(keys[3], (CLIPS, TOKENS, D), 1.0, 6.0, ((0, 4), (1, 128))),
        "out_weight": noise(keys[4], (HD, D), HD ** -0.5, 0.25),
        "memory_index": draw_memory_index(jax.random.fold_in(keys[6], 71), 0),
    }


def split_heads(matrix):
    return matrix.reshape(matrix.shape[0], HEADS, HEAD_DIM).transpose(1, 0, 2)

def merge_heads(stacked):
    return stacked.transpose(1, 0, 2).reshape(stacked.shape[1], HEADS * HEAD_DIM)

def head_pass(query_head, key_head, value_head, mem_keys, mem_values, grad_head, alive_slots):
    inv_root = 1.0 / math.sqrt(HEAD_DIM)
    keys_all = jnp.concatenate([key_head, mem_keys], 0)
    values_all = jnp.concatenate([value_head, mem_values], 0)
    scores = jnp.dot(query_head, keys_all.T, preferred_element_type=jnp.float32) * inv_root
    mask_all = jnp.concatenate([jnp.ones((key_head.shape[0],), bool), alive_slots])
    scores = jnp.where(mask_all[None, :], scores, -jnp.inf)
    row_max = lax.optimization_barrier(jnp.max(scores, axis=1, keepdims=True))
    exp_scores = jnp.exp(scores - row_max)
    soft_weights = exp_scores / lax.optimization_barrier(jnp.sum(exp_scores, axis=1, keepdims=True))
    soft_low = soft_weights.astype(jnp.bfloat16)
    attended = jnp.dot(soft_low, values_all, preferred_element_type=jnp.float32).astype(jnp.bfloat16)
    row_delta = lax.optimization_barrier(jnp.sum(grad_head.astype(jnp.float32) * attended.astype(jnp.float32), axis=1, keepdims=True))
    grad_soft = jnp.dot(grad_head, values_all.T, preferred_element_type=jnp.float32)
    grad_score = (soft_weights * (grad_soft - row_delta)).astype(jnp.bfloat16)
    grad_query = (jnp.dot(grad_score, keys_all, preferred_element_type=jnp.float32) * inv_root).astype(jnp.bfloat16)
    grad_keys = jnp.dot(grad_score.T, query_head, preferred_element_type=jnp.float32) * inv_root
    grad_values = jnp.dot(soft_low.T, grad_head, preferred_element_type=jnp.float32)
    return (attended, grad_query, grad_keys, grad_values)

def reference(query_rows, key_rows, value_rows, out_grad, out_weight, memory_index):
    slots = SEGS * MEM
    weight_total = jnp.zeros((HD, D), jnp.float32)
    query_out, key_out, value_out = ([], [], [])
    for clip in range(CLIPS):
        query_seg = query_rows[clip].reshape(SEGS, SEG, HD)
        key_seg = key_rows[clip].reshape(SEGS, SEG, HD)
        value_seg = value_rows[clip].reshape(SEGS, SEG, HD)
        grad_seg = out_grad[clip].reshape(SEGS, SEG, D)
        picked = memory_index[clip].astype(jnp.int32)
        mem_keys = jnp.take_along_axis(key_seg, picked[:, :, None], axis=1).reshape(slots, HD)
        mem_values = jnp.take_along_axis(value_seg, picked[:, :, None], axis=1).reshape(slots, HD)
        slot_segment = jnp.arange(slots, dtype=jnp.int32) // MEM

        def one_segment(carry, inputs):
            key_sum, value_sum, weight_sum = carry
            segment, query_one, key_one, value_one, grad_one = inputs
            alive_slots = slot_segment < segment
            grad_attn = jnp.dot(grad_one, out_weight.T, preferred_element_type=jnp.float32).astype(jnp.bfloat16)
            attended, grad_query, grad_keys, grad_values = jax.vmap(head_pass, in_axes=(0, 0, 0, 0, 0, 0, None))(split_heads(query_one), split_heads(key_one), split_heads(value_one), split_heads(mem_keys), split_heads(mem_values), split_heads(grad_attn), alive_slots)
            attended_rows = merge_heads(attended)
            key_all = merge_heads(grad_keys)
            value_all = merge_heads(grad_values)
            weight_sum = weight_sum + jnp.dot(attended_rows.T, grad_one, preferred_element_type=jnp.float32)
            key_sum = key_sum + key_all[SEG:]
            value_sum = value_sum + value_all[SEG:]
            return ((key_sum, value_sum, weight_sum), (merge_heads(grad_query), key_all[:SEG], value_all[:SEG]))
        start = (jnp.zeros((slots, HD), jnp.float32), jnp.zeros((slots, HD), jnp.float32), jnp.zeros((HD, D), jnp.float32))
        (key_sum, value_sum, weight_part), (grad_query, local_key, local_value) = lax.scan(one_segment, start, (jnp.arange(SEGS, dtype=jnp.int32), query_seg, key_seg, value_seg, grad_seg))
        weight_total = weight_total + weight_part

        def place(local_rows, rows_at, added):
            return local_rows.at[rows_at].add(added)
        key_full = jax.vmap(place)(local_key, picked, key_sum.reshape(SEGS, MEM, HD))
        value_full = jax.vmap(place)(local_value, picked, value_sum.reshape(SEGS, MEM, HD))
        query_out.append(grad_query.reshape(TOKENS, HD))
        key_out.append(key_full.reshape(TOKENS, HD).astype(jnp.bfloat16))
        value_out.append(value_full.reshape(TOKENS, HD).astype(jnp.bfloat16))
    weight_grad = (weight_total * (1.0 / math.sqrt(CLIPS * TOKENS))).astype(jnp.bfloat16)
    return (jnp.stack(query_out), jnp.stack(key_out), jnp.stack(value_out), weight_grad)
```

```python
import math

import jax
import jax.numpy as jnp
from jax import lax
from jax.experimental import pallas as pl
from jax.experimental.pallas import tpu as pltpu
from jax.sharding import PartitionSpec as P

HEAD_DIM = 64
SEG = 128
MEM = 8
HD = 512
D = 1024
HALF = 256
HEADS = 4
COLS = HEADS * 2 * SEG
NY, NZ, NX = 8, 8, 4
MESH = pl.DeviceIdType.MESH
F32, BF16 = jnp.float32, jnp.bfloat16

(C_IDX, C_K, C_V, C_Q, C_G, KZ, KY, VY, VZ, RKY, RKZ, RVZ, RVY, WX, WY, WZ, GZ, GY, GX, GC, O_Q, O_K, O_V) = range(23)


def nt(a, b):
    return lax.dot_general(a, b, (((1,), (1,)), ((), ())), preferred_element_type=F32)


def tn(a, b):
    return lax.dot_general(a, b, (((0,), (0,)), ((), ())), preferred_element_type=F32)


def nn(a, b):
    return jnp.dot(a, b, preferred_element_type=F32)


def rows8(block, op):
    return op(block.reshape(block.shape[0] // 8, 8, block.shape[1]), axis=0)


def kernel(
    idx_ref, q_ref, k_ref, v_ref, g_ref, w_ref,
    qo_ref, ko_ref, vo_ref, wo_ref,
    idxb, kp, vp, qp, gp, wh, q4, ga4, gat, oh, kbuf, vbuf, s_mem, s_loc,
    m8, l8, acc, qacc, kt, vt, kt_own, kg, vg, kry, krz, vrz, vry, ksum, vsum, vsum_own, krow, vrow,
    wt, wsend, wxr, wxs, wyr, wys, wzr, wg, obq, obk, obv,
    ssem, rsem, wsem,
):
    dp, tm = lax.axis_index("dp"), lax.axis_index("tm")
    c, z, y = tm % 2, (tm // 2) % NZ, tm // (2 * NZ)
    other = 1 - c

    def at_core():
        return (dp, y * 16 + z * 2 + other)

    def at_z(i):
        return (dp, y * 16 + i * 2 + c)

    def at_y(i):
        return (dp, i * 16 + z * 2 + c)

    def at_x(i):
        return (i, tm)

    def remote(src, dst, phase, mine, theirs, device):
        return pltpu.make_async_remote_copy(
            src_ref=src, dst_ref=dst, send_sem=ssem.at[phase, mine], recv_sem=rsem.at[phase, theirs],
            device_id=device, device_id_type=MESH,
        )

    def each(count, me, body):
        def step(d, _):
            body((me + d) % count)
            return 0

        lax.fori_loop(1, count, step, 0)

    def span(lo, hi, body):
        def step(i, _):
            body(i)
            return 0

        lax.fori_loop(lo, hi, step, 0)

    def blk(i):
        return pl.ds(pl.multiple_of(i * 16, 16), 16)

    my_cols = pl.ds(pl.multiple_of(c * HALF, HALF), HALF)
    their_cols = pl.ds(pl.multiple_of(other * HALF, HALF), HALF)

    vbuf[...] = jnp.zeros_like(vbuf)

    bar = pltpu.get_barrier_semaphore()

    def greet(device):
        pl.semaphore_signal(bar, inc=1, device_id=device, device_id_type=MESH)

    greet(at_core())
    each(NZ, z, lambda i: greet(at_z(i)))
    each(NY, y, lambda i: greet(at_y(i)))
    each(NX, dp, lambda i: greet(at_x(i)))

    w_copy = pltpu.make_async_copy(w_ref.at[pl.ds(pl.multiple_of(c * HALF, HALF), HALF)], wh, wsem)
    w_copy.start()

    sub = lax.broadcasted_iota(jnp.int32, (MEM, SEG), 0)
    idx = jnp.zeros((MEM, SEG), jnp.int32)
    for m in range(MEM):
        idx = jnp.where(sub == m, idx_ref[0, m], idx)
    idxb[c] = idx
    kp[c] = k_ref[:, my_cols]
    vp[c] = v_ref[:, my_cols]
    qp[c] = q_ref[:, my_cols]
    gp[c] = g_ref[...]
    vt[...] = jnp.zeros_like(vt)

    pl.semaphore_wait(bar, 1 + (NZ - 1) + (NY - 1) + (NX - 1))

    swaps = [
        remote(idxb.at[c], idxb.at[c], C_IDX, 0, 0, at_core()),
        remote(k_ref.at[:, their_cols], kp.at[c], C_K, 0, 0, at_core()),
        remote(v_ref.at[:, their_cols], vp.at[c], C_V, 0, 0, at_core()),
        remote(q_ref.at[:, their_cols], qp.at[c], C_Q, 0, 0, at_core()),
        remote(g_ref, gp.at[c], C_G, 0, 0, at_core()),
    ]
    for s in swaps:
        s.start()
    for s in swaps[:3]:
        s.wait_recv()

    lane = lax.broadcasted_iota(jnp.int32, (MEM, SEG), 1)
    zero = jnp.zeros((MEM, SEG), F32)
    one_a = jnp.where(idxb[0] == lane, 1.0, 0.0).astype(F32)
    one_b = jnp.where(idxb[1] == lane, 1.0, 0.0).astype(F32)
    oh[...] = jnp.concatenate(
        [jnp.concatenate([one_a, zero], 1), jnp.concatenate([zero, one_b], 1)], 0
    ).astype(BF16)
    k_pair = kp[...].reshape(2 * SEG, HALF)
    v_pair = vp[...].reshape(2 * SEG, HALF)
    kbuf[y, blk(z)] = nn(oh[...], k_pair).astype(BF16)
    vbuf[y, blk(z)] = nn(oh[...], v_pair).astype(BF16)

    each(NZ, z, lambda i: remote(kbuf.at[y, blk(z)], kbuf.at[y, blk(z)], KZ, i, z, at_z(i)).start())
    span(y + 1, NY, lambda i: remote(vbuf.at[y, blk(z)], vbuf.at[y, blk(z)], VY, i, y, at_y(i)).start())

    swaps[3].wait_recv()
    lanes = lax.broadcasted_iota(jnp.int32, (2 * SEG, HALF), 1) // HEAD_DIM
    q_pair = (qp[...].reshape(2 * SEG, HALF).astype(F32) * (1.0 / math.sqrt(HEAD_DIM))).astype(BF16)
    for h in range(HEADS):
        q4[pl.ds(h * 256, 256), :] = jnp.where(lanes == h, q_pair, jnp.zeros_like(q_pair))

    def score_block(keys):
        return nt(keys, q4[...])

    col = lax.broadcasted_iota(jnp.int32, (2 * SEG, COLS), 1)
    row = lax.broadcasted_iota(jnp.int32, (2 * SEG, COLS), 0)
    s = score_block(k_pair)
    s = jnp.where((row // SEG) == ((col // SEG) % 2), s, -jnp.inf)
    s_loc[...] = s
    m8[...] = rows8(s, jnp.max)

    swaps[4].wait_recv()
    w_copy.wait()
    g_pair = gp[...].reshape(2 * SEG, D)
    ga = nt(g_pair, wh[...]).astype(BF16)
    gat[...] = nt(wh[...], g_pair).astype(BF16).astype(F32)
    for h in range(HEADS):
        ga4[pl.ds(h * 256, 256), :] = jnp.where(lanes == h, ga, jnp.zeros_like(ga))

    each(NZ, z, lambda i: remote(kbuf.at[y, blk(z)], kbuf.at[y, blk(i)], KZ, i, i, at_z(i)).wait_recv())
    span(y + 1, NY, lambda i: remote(kbuf.at[y], kbuf.at[y], KY, i, y, at_y(i)).start())
    span(0, y, lambda i: remote(vbuf.at[y, blk(z)], vbuf.at[i, blk(z)], VY, i, i, at_y(i)).wait_recv())
    each(NZ, z, lambda i: remote(vbuf.at[:, blk(z)], vbuf.at[:, blk(z)], VZ, i, z, at_z(i)).start())

    def masked(block):
        at = lax.broadcasted_iota(jnp.int32, (SEG, COLS), 0) // MEM
        seg = 2 * z + (lax.broadcasted_iota(jnp.int32, (SEG, COLS), 1) // SEG) % 2
        return jnp.where(at < seg, block, -jnp.inf)

    s = masked(score_block(kbuf[y]))
    s_mem[y] = s
    m8[...] = jnp.maximum(m8[...], rows8(s, jnp.max))

    def scores_of(d):
        i = y - 1 - d
        remote(kbuf.at[y], kbuf.at[i], KY, i, i, at_y(i)).wait_recv()
        block = score_block(kbuf[i])
        s_mem[i] = block
        m8[...] = jnp.maximum(m8[...], rows8(block, jnp.max))

    span(0, y, scores_of)
    top = jnp.max(m8[...], axis=0, keepdims=True)

    def add_attended(values, p):
        p_low = p.astype(BF16)
        vals_t = values.T
        for h in range(HEADS):
            rows = pl.ds(h * HEAD_DIM, HEAD_DIM)
            acc[rows, :] = acc[rows, :] + nn(
                vals_t[h * HEAD_DIM : (h + 1) * HEAD_DIM], p_low[:, h * 256 : (h + 1) * 256]
            )

    p = jnp.exp(s_loc[...] - top)
    s_loc[...] = p
    l8[...] = rows8(p, jnp.sum)
    acc[...] = jnp.zeros_like(acc)
    add_attended(v_pair, p)
    each(NZ, z, lambda i: remote(vbuf.at[:, blk(z)], vbuf.at[:, blk(i)], VZ, i, i, at_z(i)).wait_recv())

    def soft_of(i):
        p = jnp.exp(s_mem[i] - top)
        s_mem[i] = p
        l8[...] = l8[...] + rows8(p, jnp.sum)
        add_attended(vbuf[i], p)

    span(0, y + 1, soft_of)
    inv = 1.0 / jnp.sum(l8[...], axis=0, keepdims=True)
    att = jnp.concatenate(
        [acc[h * HEAD_DIM : (h + 1) * HEAD_DIM, :] * inv[:, h * 256 : (h + 1) * 256] for h in range(HEADS)], 0
    ).astype(BF16)
    term = nn(att, g_pair)
    wt[...] = term
    wsend[...] = term.astype(BF16)

    def wrows(i):
        return pl.ds(pl.multiple_of(i * 64, 64), 64)

    each(NX, dp, lambda i: remote(wsend.at[wrows(i)], wxr.at[dp], WX, i, dp, at_x(i)).start())

    prod = att.astype(F32) * gat[...]
    delta = jnp.concatenate(
        [jnp.sum(prod[h * HEAD_DIM : (h + 1) * HEAD_DIM, :], axis=0, keepdims=True) for h in range(HEADS)], 1
    )

    def back(keys, values, p):
        pn = p * inv
        soft = nt(values, ga4[...])
        gs = (pn * (soft - delta)).astype(BF16)
        k_term = nn(gs, q4[...])
        v_term = nn(pn.astype(BF16), ga4[...])
        keys_t = keys.T
        for h in range(HEADS):
            rows = pl.ds(h * HEAD_DIM, HEAD_DIM)
            qacc[rows, :] = qacc[rows, :] + nn(
                keys_t[h * HEAD_DIM : (h + 1) * HEAD_DIM], gs[:, h * 256 : (h + 1) * 256]
            )
        return k_term, v_term

    qacc[...] = jnp.zeros_like(qacc)

    def back_of(i):
        k_term, v_term = back(kbuf[i], vbuf[i], s_mem[i])
        kt[i] = k_term.astype(BF16)
        vt[i] = v_term.astype(BF16)
        remote(kt.at[i], kry.at[y], RKY, i, y, at_y(i)).start()

    span(0, y, back_of)
    k_term, v_term = back(kbuf[y], vbuf[y], s_mem[y])
    kt_own[...] = k_term
    vt[y] = v_term.astype(BF16)
    each(NZ, z, lambda i: remote(vt.at[:, blk(i)], vrz.at[z], RVZ, i, z, at_z(i)).start())
    k_term, v_term = back(k_pair, v_pair, s_loc[...])
    kg[...] = k_term
    vg[...] = v_term
    qg = (qacc[...] * (1.0 / math.sqrt(HEAD_DIM))).T.astype(BF16)
    obq[...] = qg.reshape(2, SEG, HALF)
    qo_ref[:, my_cols] = obq[c]
    out_q = remote(obq.at[other], qo_ref.at[:, my_cols], O_Q, 0, 0, at_core())
    out_q.start()

    def add_x(i):
        remote(wsend.at[wrows(i)], wxr.at[i], WX, i, i, at_x(i)).wait_recv()
        wt[wrows(dp), :] = wt[wrows(dp), :] + wxr[i].astype(F32)

    each(NX, dp, add_x)
    wxs[...] = wt[wrows(dp), :].astype(BF16)

    def wcols(i):
        return pl.ds(pl.multiple_of(i * 128, 128), 128)

    each(NY, y, lambda i: remote(wxs.at[:, wcols(i)], wyr.at[y], WY, i, y, at_y(i)).start())

    ksum[...] = kt_own[...]

    def add_ky(i):
        remote(kt.at[0], kry.at[i], RKY, 0, i, at_y(i)).wait_recv()
        ksum[...] = ksum[...] + kry[i].astype(F32)

    span(y + 1, NY, add_ky)
    krow[...] = ksum[...].astype(BF16)
    each(NZ, z, lambda i: remote(krow.at[blk(i)], krz.at[z], RKZ, i, z, at_z(i)).start())

    vsum[...] = vt[:, blk(z)].astype(F32)

    def add_vz(i):
        remote(vt.at[:, blk(i)], vrz.at[i], RVZ, i, i, at_z(i)).wait_recv()
        vsum[...] = vsum[...] + vrz[i].astype(F32)

    each(NZ, z, add_vz)
    vrow[...] = vsum[...].astype(BF16)
    span(0, y, lambda i: remote(vrow.at[i], vry.at[y], RVY, i, y, at_y(i)).start())

    wys[...] = wt[wrows(dp), wcols(y)]

    def add_y(i):
        remote(wxs.at[:, wcols(i)], wyr.at[i], WY, i, i, at_y(i)).wait_recv()
        wys[...] = wys[...] + wyr[i].astype(F32)

    each(NY, y, add_y)

    def w8(i):
        return pl.ds(pl.multiple_of(i * 8, 8), 8)

    each(NZ, z, lambda i: remote(wys.at[w8(i)], wzr.at[z], WZ, i, z, at_z(i)).start())

    vsum_own[...] = vsum[y]

    def add_vy(i):
        remote(vrow.at[0], vry.at[i], RVY, 0, i, at_y(i)).wait_recv()
        vsum_own[...] = vsum_own[...] + vry[i].astype(F32)

    span(y + 1, NY, add_vy)
    kown = ksum.at[blk(z)]

    def add_kz(i):
        remote(krow.at[blk(i)], krz.at[i], RKZ, i, i, at_z(i)).wait_recv()
        kown[...] = kown[...] + krz[i].astype(F32)

    each(NZ, z, add_kz)

    def place(local, terms):
        hi = terms.astype(BF16)
        lo = (terms - hi.astype(F32)).astype(BF16)
        return (local + (tn(oh[...], hi) + tn(oh[...], lo))).astype(BF16).reshape(2, SEG, HALF)

    obk[...] = place(kg[...], kown[...])
    obv[...] = place(vg[...], vsum_own[...])
    out_k = remote(obk.at[other], ko_ref.at[:, my_cols], O_K, 0, 0, at_core())
    out_v = remote(obv.at[other], vo_ref.at[:, my_cols], O_V, 0, 0, at_core())
    out_k.start()
    out_v.start()
    ko_ref[:, my_cols] = obk[c]
    vo_ref[:, my_cols] = obv[c]

    wfin = wys.at[w8(z)]

    def add_z(i):
        remote(wys.at[w8(i)], wzr.at[i], WZ, i, i, at_z(i)).wait_recv()
        wfin[...] = wfin[...] + wzr[i]

    each(NZ, z, add_z)
    wg[w8(z), :] = wfin[...] * (1.0 / math.sqrt(4 * 16384))

    each(NZ, z, lambda i: remote(wg.at[w8(z)], wg.at[w8(z)], GZ, i, z, at_z(i)).start())
    each(NZ, z, lambda i: remote(wg.at[w8(z)], wg.at[w8(i)], GZ, i, i, at_z(i)).wait_recv())

    def orows(i):
        return pl.ds(pl.multiple_of(c * HALF + i * 64, 64), 64)

    wo_ref[orows(dp), wcols(y)] = wg[...].astype(BF16)
    here = wo_ref.at[orows(dp), wcols(y)]
    each(NY, y, lambda i: remote(here, here, GY, i, y, at_y(i)).start())
    each(NY, y, lambda i: remote(here, wo_ref.at[orows(dp), wcols(i)], GY, i, i, at_y(i)).wait_recv())
    mine = wo_ref.at[orows(dp)]
    each(NX, dp, lambda i: remote(mine, mine, GX, i, dp, at_x(i)).start())
    remote(mine, mine, GC, dp, dp, at_core()).start()

    def hand_on(i):
        part = wo_ref.at[orows(i)]
        remote(mine, part, GX, i, i, at_x(i)).wait_recv()
        remote(part, part, GC, i, i, at_core()).start()

    each(NX, dp, hand_on)

    def theirs(i):
        return wo_ref.at[pl.ds(pl.multiple_of(other * HALF + i * 64, 64), 64)]

    span(0, NX, lambda i: remote(theirs(i), theirs(i), GC, i, i, at_core()).wait_recv())

    out_q.wait()
    out_k.wait()
    out_v.wait()
    for s in swaps:
        s.wait_send()
    each(NZ, z, lambda i: remote(kbuf.at[y, blk(z)], kbuf.at[y, blk(z)], KZ, i, z, at_z(i)).wait_send())
    span(y + 1, NY, lambda i: remote(vbuf.at[y, blk(z)], vbuf.at[y, blk(z)], VY, i, y, at_y(i)).wait_send())
    span(y + 1, NY, lambda i: remote(kbuf.at[y], kbuf.at[y], KY, i, y, at_y(i)).wait_send())
    each(NZ, z, lambda i: remote(vbuf.at[:, blk(z)], vbuf.at[:, blk(z)], VZ, i, z, at_z(i)).wait_send())
    each(NX, dp, lambda i: remote(wsend.at[wrows(i)], wxr.at[dp], WX, i, dp, at_x(i)).wait_send())
    span(0, y, lambda i: remote(kt.at[i], kry.at[y], RKY, i, y, at_y(i)).wait_send())
    each(NZ, z, lambda i: remote(vt.at[:, blk(i)], vrz.at[z], RVZ, i, z, at_z(i)).wait_send())
    each(NY, y, lambda i: remote(wxs.at[:, wcols(i)], wyr.at[y], WY, i, y, at_y(i)).wait_send())
    each(NZ, z, lambda i: remote(krow.at[blk(i)], krz.at[z], RKZ, i, z, at_z(i)).wait_send())
    span(0, y, lambda i: remote(vrow.at[i], vry.at[y], RVY, i, y, at_y(i)).wait_send())
    each(NZ, z, lambda i: remote(wys.at[w8(i)], wzr.at[z], WZ, i, z, at_z(i)).wait_send())
    each(NZ, z, lambda i: remote(wg.at[w8(z)], wg.at[w8(z)], GZ, i, z, at_z(i)).wait_send())
    each(NY, y, lambda i: remote(here, here, GY, i, y, at_y(i)).wait_send())
    each(NX, dp, lambda i: remote(mine, mine, GX, i, dp, at_x(i)).wait_send())
    span(0, NX, lambda i: remote(wo_ref.at[orows(i)], wo_ref.at[orows(i)], GC, i, i, at_core()).wait_send())


def on_device(query_rows, key_rows, value_rows, out_grad, out_weight, memory_index):
    vmem = pl.BlockSpec(memory_space=pltpu.VMEM)
    V = pltpu.VMEM
    scratch = [
        V((2, MEM, SEG), jnp.int32),
        V((2, SEG, HALF), BF16), V((2, SEG, HALF), BF16), V((2, SEG, HALF), BF16),
        V((2, SEG, D), BF16), V((HALF, D), BF16),
        V((COLS, HALF), BF16), V((COLS, HALF), BF16), V((HALF, HALF), F32),
        V((16, HALF), BF16),
        V((NY, SEG, HALF), BF16), V((NY, SEG, HALF), BF16),
        V((NY, SEG, COLS), F32), V((2 * SEG, COLS), F32),
        V((8, COLS), F32), V((8, COLS), F32),
        V((HALF, HALF), F32), V((HALF, HALF), F32),
        V((NY, SEG, HALF), BF16), V((NY, SEG, HALF), BF16), V((SEG, HALF), F32),
        V((HALF, HALF), F32), V((HALF, HALF), F32),
        V((NY, SEG, HALF), BF16), V((NZ, 16, HALF), BF16),
        V((NZ, NY, 16, HALF), BF16), V((NY, 16, HALF), BF16),
        V((SEG, HALF), F32), V((NY, 16, HALF), F32), V((16, HALF), F32),
        V((SEG, HALF), BF16), V((NY, 16, HALF), BF16),
        V((HALF, D), F32), V((HALF, D), BF16),
        V((NX, 64, D), BF16), V((64, D), BF16),
        V((NY, 64, 128), BF16), V((64, 128), F32),
        V((NZ, 8, 128), F32), V((64, 128), F32),
        V((2, SEG, HALF), BF16), V((2, SEG, HALF), BF16), V((2, SEG, HALF), BF16),
        pltpu.SemaphoreType.DMA((23, 8)), pltpu.SemaphoreType.DMA((23, 8)), pltpu.SemaphoreType.DMA(()),
    ]
    qg, kgrad, vgrad, wgrad = pl.pallas_call(
        kernel,
        out_shape=(
            jax.ShapeDtypeStruct((SEG, HD), BF16),
            jax.ShapeDtypeStruct((SEG, HD), BF16),
            jax.ShapeDtypeStruct((SEG, HD), BF16),
            jax.ShapeDtypeStruct((HD, D), BF16),
        ),
        in_specs=[pl.BlockSpec(memory_space=pltpu.SMEM), vmem, vmem, vmem, vmem, pl.BlockSpec(memory_space=pl.ANY)],
        out_specs=(vmem, vmem, vmem, vmem),
        scratch_shapes=scratch,
        compiler_params=pltpu.CompilerParams(
            collective_id=0, has_side_effects=True, vmem_limit_bytes=48 * 2**20
        ),
        name="memory_attention_backward",
    )(memory_index[0], query_rows[0], key_rows[0], value_rows[0], out_grad[0], out_weight)
    return qg[None], kgrad[None], vgrad[None], wgrad


def solution(mesh):
    placed = (
        P("dp", "tm", None),
        P("dp", "tm", None),
        P("dp", "tm", None),
        P("dp", "tm", None),
        P(),
        P("dp", "tm", None),
    )
    return jax.shard_map(
        on_device,
        mesh=mesh,
        in_specs=placed,
        out_specs=(P("dp", "tm", None), P("dp", "tm", None), P("dp", "tm", None), P()),
        check_vma=False,
    )
```

```python
import math

import jax
import jax.numpy as jnp
from jax import lax
from jax.experimental import pallas as pl
from jax.experimental.pallas import tpu as pltpu
from jax.sharding import PartitionSpec as P

HEAD_DIM = 64
SEG = 128
MEM = 8
HD = 512
D = 1024
HALF = 256
HEADS = 4
COLS = HEADS * 2 * SEG
NY, NZ, NX = 8, 8, 4
MESH = pl.DeviceIdType.MESH
F32, BF16 = jnp.float32, jnp.bfloat16

(
    C_IDX, C_K, C_V, C_Q, C_G, KZ, KU, KU1, KD, KD1, VY, VU, VU1, VD, VD1,
    RKY, RKZ, RVZ, RVZ1, RVY, WX, WY, WZ, GY, GC, GD, O_Q, O_K, O_V, GX,
) = range(30)
PHASES = GX + NX


def nt(a, b):
    return lax.dot_general(a, b, (((1,), (1,)), ((), ())), preferred_element_type=F32)


def tn(a, b):
    return lax.dot_general(a, b, (((0,), (0,)), ((), ())), preferred_element_type=F32)


def nn(a, b):
    return jnp.dot(a, b, preferred_element_type=F32)


def rows8(block, op):
    return op(block.reshape(block.shape[0] // 8, 8, block.shape[1]), axis=0)


def kernel(
    idx_in, q_ref, k_ref, v_ref, g_ref, w_ref,
    qo_ref, ko_ref, vo_ref, wout_ref,
    idx_ref, idxb, kp, vp, qp, gp, wh, q4, ga4, gat, oh, kbuf, vbuf, s_mem, s_loc,
    m8, l8, acc, qacc, kt, vt, kg, vg, kry, krz, vrz, vry, ksum, vsum, vsum_own, krow, vrow,
    wt, wsend, wxr, wxs, wyr, wys, wzr, wo_ref, obq, obk, obv,
    ssem, rsem, lsem,
):
    dp, tm = lax.axis_index("dp"), lax.axis_index("tm")
    c, z, y = tm % 2, (tm // 2) % NZ, tm // (2 * NZ)
    other = 1 - c

    def at_core():
        return (dp, y * 16 + z * 2 + other)

    def at_z(i):
        return (dp, y * 16 + i * 2 + c)

    def at_y(i):
        return (dp, i * 16 + z * 2 + c)

    def at_x(i):
        return (i, tm)

    def remote(src, dst, phase, mine, theirs, device):
        return pltpu.make_async_remote_copy(
            src_ref=src, dst_ref=dst, send_sem=ssem.at[phase, mine], recv_sem=rsem.at[phase, theirs],
            device_id=device, device_id_type=MESH,
        )

    def each(count, me, body):
        def step(d, _):
            body((me + d) % count)
            return 0

        lax.fori_loop(1, count, step, 0)

    def span(lo, hi, body):
        def step(i, _):
            body(i)
            return 0

        lax.fori_loop(lo, hi, step, 0)

    def blk(i):
        return pl.ds(pl.multiple_of(i * 16, 16), 16)

    my_cols = pl.ds(pl.multiple_of(c * HALF, HALF), HALF)
    their_cols = pl.ds(pl.multiple_of(other * HALF, HALF), HALF)

    kbuf[...] = jnp.zeros_like(kbuf)
    vbuf[...] = jnp.zeros_like(vbuf)

    local = [
        pltpu.make_async_copy(src, dst, lsem.at[i])
        for i, (src, dst) in enumerate((
            (idx_in.at[0], idx_ref),
            (k_ref.at[:, my_cols], kp.at[c]),
            (v_ref.at[:, my_cols], vp.at[c]),
            (q_ref.at[:, my_cols], qp.at[c]),
            (g_ref, gp.at[c]),
            (w_ref.at[pl.ds(pl.multiple_of(c * HALF, HALF), HALF)], wh),
        ))
    ]
    for copy in local:
        copy.start()

    bar = pltpu.get_barrier_semaphore()

    def greet(device):
        pl.semaphore_signal(bar, inc=1, device_id=device, device_id_type=MESH)

    greet(at_core())
    each(NZ, z, lambda i: greet(at_z(i)))
    each(NY, y, lambda i: greet(at_y(i)))
    each(NX, dp, lambda i: greet(at_x(i)))

    vt[...] = jnp.zeros_like(vt)
    pl.semaphore_wait(bar, 1 + (NZ - 1) + (NY - 1) + (NX - 1))

    swaps = [
        remote(idxb.at[c], idxb.at[c], C_IDX, 0, 0, at_core()),
        remote(k_ref.at[:, their_cols], kp.at[c], C_K, 0, 0, at_core()),
        remote(v_ref.at[:, their_cols], vp.at[c], C_V, 0, 0, at_core()),
        remote(q_ref.at[:, their_cols], qp.at[c], C_Q, 0, 0, at_core()),
        remote(g_ref, gp.at[c], C_G, 0, 0, at_core()),
    ]
    swaps[1].start()
    swaps[2].start()
    local[0].wait()
    sub = lax.broadcasted_iota(jnp.int32, (MEM, SEG), 0)
    idx = jnp.zeros((MEM, SEG), jnp.int32)
    for m in range(MEM):
        idx = jnp.where(sub == m, idx_ref[m], idx)
    idxb[c] = idx
    swaps[0].start()
    swaps[3].start()
    swaps[4].start()
    local[1].wait()
    local[2].wait()
    for s in swaps[:3]:
        s.wait_recv()

    lane = lax.broadcasted_iota(jnp.int32, (MEM, SEG), 1)
    zero = jnp.zeros((MEM, SEG), F32)
    one_a = jnp.where(idxb[0] == lane, 1.0, 0.0).astype(F32)
    one_b = jnp.where(idxb[1] == lane, 1.0, 0.0).astype(F32)
    oh[...] = jnp.concatenate(
        [jnp.concatenate([one_a, zero], 1), jnp.concatenate([zero, one_b], 1)], 0
    ).astype(BF16)
    k_pair = kp[...].reshape(2 * SEG, HALF)
    v_pair = vp[...].reshape(2 * SEG, HALF)
    kbuf[y, blk(z)] = nn(oh[...], k_pair).astype(BF16)
    vbuf[y, blk(z)] = nn(oh[...], v_pair).astype(BF16)

    each(NZ, z, lambda i: remote(kbuf.at[y, blk(z)], kbuf.at[y, blk(z)], KZ, i, z, at_z(i)).start())
    span(y + 1, NY, lambda i: remote(vbuf.at[y, blk(z)], vbuf.at[y, blk(z)], VY, i, y, at_y(i)).start())

    local[3].wait()
    swaps[3].wait_recv()
    lanes = lax.broadcasted_iota(jnp.int32, (2 * SEG, HALF), 1) // HEAD_DIM
    q_pair = (qp[...].reshape(2 * SEG, HALF).astype(F32) * (1.0 / math.sqrt(HEAD_DIM))).astype(BF16)
    for h in range(HEADS):
        q4[pl.ds(h * 256, 256), :] = jnp.where(lanes == h, q_pair, jnp.zeros_like(q_pair))

    def score_block(keys):
        return nt(keys, q4[...])

    col = lax.broadcasted_iota(jnp.int32, (2 * SEG, COLS), 1)
    row = lax.broadcasted_iota(jnp.int32, (2 * SEG, COLS), 0)
    s = score_block(k_pair)
    s = jnp.where((row // SEG) == ((col // SEG) % 2), s, -jnp.inf)
    s_loc[...] = s
    m8[...] = rows8(s, jnp.max)

    local[4].wait()
    local[5].wait()
    swaps[4].wait_recv()
    g_pair = gp[...].reshape(2 * SEG, D)
    ga = nt(g_pair, wh[...]).astype(BF16)
    gat[...] = nt(wh[...], g_pair).astype(BF16).astype(F32)
    for h in range(HEADS):
        ga4[pl.ds(h * 256, 256), :] = jnp.where(lanes == h, ga, jnp.zeros_like(ga))

    each(NZ, z, lambda i: remote(kbuf.at[y, blk(z)], kbuf.at[y, blk(i)], KZ, i, i, at_z(i)).wait_recv())

    up_y, dn_y, up_z, dn_z = (y + 1) % NY, (y + NY - 1) % NY, (z + 1) % NZ, (z + NZ - 1) % NZ

    def k_pass(phase, device, b, part):
        ref = kbuf.at[b, pl.ds(part * 64, 64)]
        return remote(ref, ref, phase + part, b, b, device)

    def v_pass(phase, device, b, part):
        ref = vbuf.at[pl.ds(part * 4, 4), blk(b)]
        return remote(ref, ref, phase + part, b, b, device)

    def k_up(b, part):
        return k_pass(KU, at_y(up_y), b, part)

    def k_dn(b, part):
        return k_pass(KD, at_y(dn_y), b, part)

    def v_up(b, part):
        return v_pass(VU, at_z(up_z), b, part)

    def v_dn(b, part):
        return v_pass(VD, at_z(dn_z), b, part)

    def begin(copy, b):
        copy(b, 0).start()
        copy(b, 1).start()

    def hand_on(copy, b, more):
        for part in range(2):
            copy(b, part).wait_recv()

            @pl.when(more)
            def _():
                copy(b, part).start()

    @pl.when(y < NY - 1)
    def _():
        begin(k_up, y)

    @pl.when(y <= 2)
    def _():
        begin(k_dn, y)

    span(0, y, lambda i: remote(vbuf.at[y, blk(z)], vbuf.at[i, blk(z)], VY, i, i, at_y(i)).wait_recv())
    begin(v_up, z)
    begin(v_dn, z)

    def masked(block):
        at = lax.broadcasted_iota(jnp.int32, (SEG, COLS), 0) // MEM
        seg = 2 * z + (lax.broadcasted_iota(jnp.int32, (SEG, COLS), 1) // SEG) % 2
        return jnp.where(at < seg, block, -jnp.inf)

    s = masked(score_block(kbuf[y]))
    s_mem[y] = s
    m8[...] = jnp.maximum(m8[...], rows8(s, jnp.max))

    def scores_of(i):
        block = score_block(kbuf[i])
        s_mem[i] = block
        m8[...] = jnp.maximum(m8[...], rows8(block, jnp.max))

    def gather_step(step):
        below, above = y - step, (y + step) % NY
        from_above = (step <= 3) & (above <= 2)

        @pl.when(below >= 0)
        def _():
            hand_on(k_up, below, (step < 4) & (y < NY - 1))

        @pl.when(from_above)
        def _():
            hand_on(k_dn, above, step < 3)

        hand_on(v_up, (z + NZ - step) % NZ, step < 4)

        @pl.when(step <= 3)
        def _():
            hand_on(v_dn, (z + step) % NZ, step < 3)

        @pl.when(below >= 0)
        def _():
            scores_of(below)

        @pl.when(from_above & (above < y))
        def _():
            scores_of(above)

    span(1, 5, gather_step)
    pairs = y // 2 + 1

    @pl.when(y % 2 == 0)
    def _():
        s_mem[y + 1] = jnp.full((SEG, COLS), -jnp.inf, F32)

    def two(i):
        return pl.ds(2 * i, 2)

    top = jnp.max(m8[...], axis=0, keepdims=True)

    def add_attended(values, p):
        p_low = p.astype(BF16)
        vals_t = values.T
        for h in range(HEADS):
            rows = pl.ds(h * HEAD_DIM, HEAD_DIM)
            acc[rows, :] = acc[rows, :] + nn(
                vals_t[h * HEAD_DIM : (h + 1) * HEAD_DIM], p_low[:, h * 256 : (h + 1) * 256]
            )

    p = jnp.exp(s_loc[...] - top)
    s_loc[...] = p
    l8[...] = rows8(p, jnp.sum)
    acc[...] = jnp.zeros_like(acc)
    add_attended(v_pair, p)

    def soft_of(i):
        p = jnp.exp(s_mem[two(i)].reshape(2 * SEG, COLS) - top)
        s_mem[two(i)] = p.reshape(2, SEG, COLS)
        l8[...] = l8[...] + rows8(p, jnp.sum)
        add_attended(vbuf[two(i)].reshape(2 * SEG, HALF), p)

    span(0, pairs, soft_of)
    inv = 1.0 / jnp.sum(l8[...], axis=0, keepdims=True)
    att = jnp.concatenate(
        [acc[h * HEAD_DIM : (h + 1) * HEAD_DIM, :] * inv[:, h * 256 : (h + 1) * 256] for h in range(HEADS)], 0
    ).astype(BF16)
    term = nn(att, g_pair)
    wt[...] = term
    wsend[...] = term.astype(BF16)

    def wrows(i):
        return pl.ds(pl.multiple_of(i * 64, 64), 64)

    each(NX, dp, lambda i: remote(wsend.at[wrows(i)], wxr.at[dp], WX, i, dp, at_x(i)).start())

    prod = att.astype(F32) * gat[...]
    delta = jnp.concatenate(
        [jnp.sum(prod[h * HEAD_DIM : (h + 1) * HEAD_DIM, :], axis=0, keepdims=True) for h in range(HEADS)], 1
    )

    def back(keys, values, p):
        pn = p * inv
        soft = nt(values, ga4[...])
        gs = (pn * (soft - delta)).astype(BF16)
        k_term = nn(gs, q4[...])
        v_term = nn(pn.astype(BF16), ga4[...])
        keys_t = keys.T
        for h in range(HEADS):
            rows = pl.ds(h * HEAD_DIM, HEAD_DIM)
            qacc[rows, :] = qacc[rows, :] + nn(
                keys_t[h * HEAD_DIM : (h + 1) * HEAD_DIM], gs[:, h * 256 : (h + 1) * 256]
            )
        return k_term, v_term

    qacc[...] = jnp.zeros_like(qacc)

    def back_of(i):
        k_term, v_term = back(
            kbuf[two(i)].reshape(2 * SEG, HALF), vbuf[two(i)].reshape(2 * SEG, HALF),
            s_mem[two(i)].reshape(2 * SEG, COLS),
        )
        kt[two(i)] = k_term.astype(BF16).reshape(2, SEG, HALF)
        vt[two(i)] = v_term.astype(BF16).reshape(2, SEG, HALF)
        for j in (2 * i, 2 * i + 1):
            @pl.when(j < y)
            def _():
                remote(kt.at[j], kry.at[y], RKY, j, y, at_y(j)).start()

        @pl.when(i == 1)
        def _():
            v_half(0)

    def v_send(half, i):
        part = pl.ds(half * 4, 4)
        return remote(vt.at[part, blk(i)], vrz.at[z, part], RVZ + half, i, z, at_z(i))

    def v_half(half):
        each(NZ, z, lambda i: v_send(half, i).start())

    span(0, pairs, back_of)

    @pl.when(y < 2)
    def _():
        v_half(0)

    @pl.when(y >= 4)
    def _():
        v_half(1)

    k_term, v_term = back(k_pair, v_pair, s_loc[...])
    kg[...] = k_term
    vg[...] = v_term
    qg = (qacc[...] * (1.0 / math.sqrt(HEAD_DIM))).T.astype(BF16)
    obq[...] = qg.reshape(2, SEG, HALF)
    out_q = remote(obq.at[other], qo_ref.at[:, my_cols], O_Q, 0, 0, at_core())
    out_q.start()
    keep_q = pltpu.make_async_copy(obq.at[c], qo_ref.at[:, my_cols], lsem.at[6])
    keep_q.start()

    def add_x(i):
        remote(wsend.at[wrows(i)], wxr.at[i], WX, i, i, at_x(i)).wait_recv()
        wt[wrows(dp), :] = wt[wrows(dp), :] + wxr[i].astype(F32)

    each(NX, dp, add_x)
    wxs[...] = wt[wrows(dp), :].astype(BF16)

    def wcols(i):
        return pl.ds(pl.multiple_of(i * 128, 128), 128)

    each(NY, y, lambda i: remote(wxs.at[:, wcols(i)], wyr.at[y], WY, i, y, at_y(i)).start())

    def add_vz(half):
        part = pl.ds(half * 4, 4)
        vsum[part] = vt[part, blk(z)].astype(F32)

        def add(i):
            v_send(half, i).wait_send()
            remote(vt.at[part, blk(i)], vrz.at[i, part], RVZ + half, i, i, at_z(i)).wait_recv()
            vsum[part] = vsum[part] + vrz[i, part].astype(F32)

        each(NZ, z, add)

    add_vz(0)

    @pl.when(y >= 4)
    def _():
        add_vz(1)

    vrow[...] = vsum[...].astype(BF16)
    span(0, y, lambda i: remote(vrow.at[i], vry.at[y], RVY, i, y, at_y(i)).start())

    wys[...] = wt[wrows(dp), wcols(y)]

    def add_y(i):
        remote(wxs.at[:, wcols(i)], wyr.at[i], WY, i, i, at_y(i)).wait_recv()
        wys[...] = wys[...] + wyr[i].astype(F32)

    each(NY, y, add_y)
    wzr[z] = wys[...].astype(BF16)
    each(NZ, z, lambda i: remote(wzr.at[z], wzr.at[z], WZ, i, z, at_z(i)).start())

    ksum[...] = kt[y].astype(F32)

    def add_ky(i):
        remote(kt.at[0], kry.at[i], RKY, 0, i, at_y(i)).wait_recv()
        ksum[...] = ksum[...] + kry[i].astype(F32)

    span(y + 1, NY, add_ky)
    krow[...] = ksum[...].astype(BF16)
    each(NZ, z, lambda i: remote(krow.at[blk(i)], krz.at[z], RKZ, i, z, at_z(i)).start())

    each(NZ, z, lambda i: remote(wzr.at[z], wzr.at[i], WZ, i, i, at_z(i)).wait_recv())
    total = wzr[0].astype(F32)
    for i in range(1, NZ):
        total = total + wzr[i].astype(F32)

    def piece(i, j):
        return wo_ref.at[wrows(i), wcols(j)]

    def out_rows(half, i):
        return wout_ref.at[pl.ds(pl.multiple_of(half * HALF + i * 64, 64), 64)]

    def out_piece(half, i, j):
        return wout_ref.at[pl.ds(pl.multiple_of(half * HALF + i * 64, 64), 64), wcols(j)]

    wo_ref[wrows(dp), wcols(y)] = (total * (1.0 / math.sqrt(4 * 16384))).astype(BF16)
    here = piece(dp, y)

    def send_x(i, j):
        return pltpu.make_async_remote_copy(
            src_ref=piece(dp, j), dst_ref=piece(dp, j), send_sem=ssem.at[GX + i, j], recv_sem=rsem.at[GX + dp, j],
            device_id=at_x(i), device_id_type=MESH,
        )

    def to_x(j):
        each(NX, dp, lambda i: send_x(i, j).start())
        remote(piece(dp, j), out_piece(c, dp, j), GC, j, j, at_core()).start()

    def keep(i):
        return pltpu.make_async_copy(wo_ref.at[wrows(i)], out_rows(c, i), lsem.at[9 + i])

    each(NY, y, lambda i: remote(here, here, GY, i, y, at_y(i)).start())
    to_x(y)

    def from_y(i):
        remote(here, piece(dp, i), GY, i, i, at_y(i)).wait_recv()
        to_x(i)

    each(NY, y, from_y)
    keep(dp).start()

    vsum_own[...] = vsum[y]

    def add_vy(i):
        remote(vrow.at[0], vry.at[i], RVY, 0, i, at_y(i)).wait_recv()
        vsum_own[...] = vsum_own[...] + vry[i].astype(F32)

    span(y + 1, NY, add_vy)
    kown = ksum.at[blk(z)]

    def add_kz(i):
        remote(krow.at[blk(i)], krz.at[i], RKZ, i, i, at_z(i)).wait_recv()
        kown[...] = kown[...] + krz[i].astype(F32)

    each(NZ, z, add_kz)

    def place(local, terms):
        hi = terms.astype(BF16)
        lo = (terms - hi.astype(F32)).astype(BF16)
        return (local + (tn(oh[...], hi) + tn(oh[...], lo))).astype(BF16).reshape(2, SEG, HALF)

    obk[...] = place(kg[...], kown[...])
    obv[...] = place(vg[...], vsum_own[...])
    out_k = remote(obk.at[other], ko_ref.at[:, my_cols], O_K, 0, 0, at_core())
    out_v = remote(obv.at[other], vo_ref.at[:, my_cols], O_V, 0, 0, at_core())
    out_k.start()
    out_v.start()
    keep_k = pltpu.make_async_copy(obk.at[c], ko_ref.at[:, my_cols], lsem.at[7])
    keep_v = pltpu.make_async_copy(obv.at[c], vo_ref.at[:, my_cols], lsem.at[8])
    keep_k.start()
    keep_v.start()

    def from_x(i):
        span(0, NY, lambda j: remote(piece(i, j), piece(i, j), GX + i, j, j, at_x(i)).wait_recv())
        remote(wo_ref.at[wrows(i)], out_rows(c, i), GD, i, i, at_core()).start()
        keep(i).start()

    each(NX, dp, from_x)
    span(0, NY, lambda j: remote(here, out_piece(other, dp, j), GC, j, j, at_core()).wait_recv())
    each(NX, dp, lambda i: remote(wo_ref.at[wrows(i)], out_rows(other, i), GD, i, i, at_core()).wait_recv())
    span(0, NX, lambda i: keep(i).wait())
    keep_q.wait()
    keep_k.wait()
    keep_v.wait()

    out_q.wait()
    out_k.wait()
    out_v.wait()
    for s in swaps:
        s.wait_send()
    each(NZ, z, lambda i: remote(kbuf.at[y, blk(z)], kbuf.at[y, blk(z)], KZ, i, z, at_z(i)).wait_send())
    span(y + 1, NY, lambda i: remote(vbuf.at[y, blk(z)], vbuf.at[y, blk(z)], VY, i, y, at_y(i)).wait_send())

    def sent(copy, b):
        copy(b, 0).wait_send()
        copy(b, 1).wait_send()

    def gather_sent(step):
        below, above = y - step, (y + step) % NY

        @pl.when((below >= 0) & (step < 4) & (y < NY - 1))
        def _():
            sent(k_up, below)

        @pl.when((step < 3) & (above <= 2))
        def _():
            sent(k_dn, above)

        sent(v_up, (z + NZ - step) % NZ)

        @pl.when(step < 3)
        def _():
            sent(v_dn, (z + step) % NZ)

    span(0, 4, gather_sent)
    each(NX, dp, lambda i: remote(wsend.at[wrows(i)], wxr.at[dp], WX, i, dp, at_x(i)).wait_send())
    span(0, y, lambda i: remote(kt.at[i], kry.at[y], RKY, i, y, at_y(i)).wait_send())
    each(NY, y, lambda i: remote(wxs.at[:, wcols(i)], wyr.at[y], WY, i, y, at_y(i)).wait_send())
    each(NZ, z, lambda i: remote(krow.at[blk(i)], krz.at[z], RKZ, i, z, at_z(i)).wait_send())
    span(0, y, lambda i: remote(vrow.at[i], vry.at[y], RVY, i, y, at_y(i)).wait_send())
    each(NZ, z, lambda i: remote(wzr.at[z], wzr.at[z], WZ, i, z, at_z(i)).wait_send())
    each(NY, y, lambda i: remote(here, here, GY, i, y, at_y(i)).wait_send())
    span(0, NY, lambda j: remote(piece(dp, j), out_piece(c, dp, j), GC, j, j, at_core()).wait_send())

    def x_sent(i):
        span(0, NY, lambda j: send_x(i, j).wait_send())
        remote(wo_ref.at[wrows(i)], out_rows(c, i), GD, i, i, at_core()).wait_send()

    each(NX, dp, x_sent)


def store(*refs):
    arrays, outs, held, sem = refs[:4], refs[4:8], refs[8:12], refs[12]
    loads = [pltpu.make_async_copy(arrays[i], held[i], sem.at[0, i]) for i in range(4)]
    stores = [pltpu.make_async_copy(held[i], outs[i], sem.at[1, i]) for i in range(4)]
    for copy in loads:
        copy.start()
    for load, copy in zip(loads, stores):
        load.wait()
        copy.start()
    for copy in stores:
        copy.wait()


def on_device(query_rows, key_rows, value_rows, out_grad, out_weight, memory_index):
    V = pltpu.VMEM
    scratch = [
        pltpu.SMEM((MEM,), jnp.int32), V((2, MEM, SEG), jnp.int32),
        V((2, SEG, HALF), BF16), V((2, SEG, HALF), BF16), V((2, SEG, HALF), BF16),
        V((2, SEG, D), BF16), V((HALF, D), BF16),
        V((COLS, HALF), BF16), V((COLS, HALF), BF16), V((HALF, HALF), F32),
        V((16, HALF), BF16),
        V((NY, SEG, HALF), BF16), V((NY, SEG, HALF), BF16),
        V((NY, SEG, COLS), F32), V((2 * SEG, COLS), F32),
        V((8, COLS), F32), V((8, COLS), F32),
        V((HALF, HALF), F32), V((HALF, HALF), F32),
        V((NY, SEG, HALF), BF16), V((NY, SEG, HALF), BF16),
        V((HALF, HALF), F32), V((HALF, HALF), F32),
        V((NY, SEG, HALF), BF16), V((NZ, 16, HALF), BF16),
        V((NZ, NY, 16, HALF), BF16), V((NY, 16, HALF), BF16),
        V((SEG, HALF), F32), V((NY, 16, HALF), F32), V((16, HALF), F32),
        V((SEG, HALF), BF16), V((NY, 16, HALF), BF16),
        V((HALF, D), F32), V((HALF, D), BF16),
        V((NX, 64, D), BF16), V((64, D), BF16),
        V((NY, 64, 128), BF16), V((64, 128), F32),
        V((NZ, 64, 128), BF16), V((HALF, D), BF16),
        V((2, SEG, HALF), BF16), V((2, SEG, HALF), BF16), V((2, SEG, HALF), BF16),
        pltpu.SemaphoreType.DMA((PHASES, 8)), pltpu.SemaphoreType.DMA((PHASES, 8)), pltpu.SemaphoreType.DMA((9 + NX,)),
    ]
    qg, kgrad, vgrad, wgrad = pl.pallas_call(
        kernel,
        out_shape=(
            jax.ShapeDtypeStruct((SEG, HD), BF16),
            jax.ShapeDtypeStruct((SEG, HD), BF16),
            jax.ShapeDtypeStruct((SEG, HD), BF16),
            jax.ShapeDtypeStruct((HD, D), BF16),
        ),
        in_specs=[pl.BlockSpec(memory_space=pltpu.HBM)] * 6,
        out_specs=[pl.BlockSpec(memory_space=pltpu.HBM)] * 4,
        scratch_shapes=scratch,
        compiler_params=pltpu.CompilerParams(
            collective_id=0, has_side_effects=True, vmem_limit_bytes=64 * 2**20
        ),
        name="memory_attention_backward",
    )(memory_index[0], query_rows[0], key_rows[0], value_rows[0], out_grad[0], out_weight)
    qg, kgrad, vgrad, wgrad = pl.pallas_call(
        store,
        out_shape=tuple(jax.ShapeDtypeStruct(a.shape, a.dtype) for a in (qg, kgrad, vgrad, wgrad)),
        in_specs=[pl.BlockSpec(memory_space=pltpu.HBM)] * 4,
        compiler_params=pltpu.CompilerParams(vmem_limit_bytes=64 * 2**20),
        out_specs=[pl.BlockSpec(memory_space=pltpu.HBM)] * 4,
        scratch_shapes=[V((SEG, HD), BF16)] * 3 + [V((HD, D), BF16), pltpu.SemaphoreType.DMA((2, 4))],
        name="store_results",
    )(qg, kgrad, vgrad, wgrad)
    return qg[None], kgrad[None], vgrad[None], wgrad


def solution(mesh):
    placed = (
        P("dp", "tm", None),
        P("dp", "tm", None),
        P("dp", "tm", None),
        P("dp", "tm", None),
        P(),
        P("dp", "tm", None),
    )
    return jax.shard_map(
        on_device,
        mesh=mesh,
        in_specs=placed,
        out_specs=(P("dp", "tm", None), P("dp", "tm", None), P("dp", "tm", None), P()),
        check_vma=False,
    )
```

```python
import math

import jax
import jax.numpy as jnp
from jax import lax
from jax.experimental import pallas as pl
from jax.experimental.pallas import tpu as pltpu
from jax.sharding import PartitionSpec as P

HEAD_DIM = 64
SEG = 128
MEM = 8
HD = 512
D = 1024
HALF = 256
HEADS = 4
COLS = HEADS * 2 * SEG
NY, NZ, NX = 8, 8, 4
MESH = pl.DeviceIdType.MESH
F32, BF16 = jnp.float32, jnp.bfloat16

PARTS = 2
(
    C_IDX, C_K, C_V, C_Q, C_G, KZ, KU, KD, VY, VU, VD, RKY, RKZ, RVZ, RVZ1, RVY,
    WX, WY, WZ, GY, GX, GR, GC, GD, O_Q, O_K, O_V,
) = range(27)
COUNTS = [(1, 1)] * 27
COUNTS[KU], COUNTS[KD], COUNTS[VU], COUNTS[VD] = (4 * PARTS,) * 2, (3 * PARTS,) * 2, (1, 4 * PARTS), (1, 3 * PARTS)
COUNTS[VY] = COUNTS[RKY] = COUNTS[RVY] = (NY, NY)
COUNTS[GY], COUNTS[GX] = (1, NY), (NX, 7)
SENDS = [sum(n for n, _ in COUNTS[:i]) for i in range(28)]
ARRIVALS = [sum(n for _, n in COUNTS[:i]) for i in range(28)]
FROM_RIGHT, FROM_LEFT, FROM_ACROSS = 0, 5, 6


def nt(a, b):
    return lax.dot_general(a, b, (((1,), (1,)), ((), ())), preferred_element_type=F32)


def tn(a, b):
    return lax.dot_general(a, b, (((0,), (0,)), ((), ())), preferred_element_type=F32)


def nn(a, b):
    return jnp.dot(a, b, preferred_element_type=F32)


def rows8(block, op):
    return op(block.reshape(block.shape[0] // 8, 8, block.shape[1]), axis=0)


def kernel(
    idx_in, q_ref, k_ref, v_ref, g_ref, w_ref,
    qo_ref, ko_ref, vo_ref, wout_ref,
    idx_ref, idxb, kp, vp, qp, gp, wh, q4, ga4, gat, oh, kbuf, vbuf, s_mem, s_loc,
    m8, l8, acc, qacc, kt, vt, kg, vg, kry, krz, vrz, vry, ksum, vsum, vsum_own, krow, vrow,
    wt, wsend, wxr, wxs, wyr, wys, wzr, wo_ref, obq, obk, obv,
    ssem, rsem, lsem,
):
    dp, tm = lax.axis_index("dp"), lax.axis_index("tm")
    c, z, y = tm % 2, (tm // 2) % NZ, tm // (2 * NZ)
    other = 1 - c

    def at_core():
        return (dp, y * 16 + z * 2 + other)

    def at_z(i):
        return (dp, y * 16 + i * 2 + c)

    def at_y(i):
        return (dp, i * 16 + z * 2 + c)

    def at_x(i):
        return (i, tm)

    def remote(src, dst, phase, mine, theirs, device):
        return pltpu.make_async_remote_copy(
            src_ref=src, dst_ref=dst, send_sem=ssem.at[SENDS[phase] + mine],
            recv_sem=rsem.at[ARRIVALS[phase] + theirs],
            device_id=device, device_id_type=MESH,
        )

    def far(count, k):
        return count // 2 + (1 - 2 * (k % 2)) * ((k + 1) // 2)

    def arrived(ref, phase, at=0):
        remote(ref, ref, phase, 0, at, at_core()).wait_recv()

    def left(ref, phase, at=0):
        remote(ref, ref, phase, at, 0, at_core()).wait_send()

    def each(count, me, body, near=False):
        def step(k, _):
            body((me + far(count, count - 2 - k if near else k)) % count)
            return 0

        lax.fori_loop(0, count - 1, step, 0)

    def span(lo, hi, body):
        def step(i, _):
            body(i)
            return 0

        lax.fori_loop(lo, hi, step, 0)

    def blk(i):
        return pl.ds(pl.multiple_of(i * 16, 16), 16)

    my_cols = pl.ds(pl.multiple_of(c * HALF, HALF), HALF)
    their_cols = pl.ds(pl.multiple_of(other * HALF, HALF), HALF)

    kbuf[...] = jnp.zeros_like(kbuf)
    vbuf[...] = jnp.zeros_like(vbuf)

    local = [
        pltpu.make_async_copy(src, dst, lsem.at[i])
        for i, (src, dst) in enumerate((
            (idx_in.at[0], idx_ref),
            (k_ref.at[:, my_cols], kp.at[c]),
            (v_ref.at[:, my_cols], vp.at[c]),
            (q_ref.at[:, my_cols], qp.at[c]),
            (g_ref, gp.at[c]),
            (w_ref.at[pl.ds(pl.multiple_of(c * HALF, HALF), HALF)], wh),
        ))
    ]
    for copy in local:
        copy.start()

    bar = pltpu.get_barrier_semaphore()

    def greet(device):
        pl.semaphore_signal(bar, inc=1, device_id=device, device_id_type=MESH)

    greet(at_core())
    each(NZ, z, lambda i: greet(at_z(i)))
    each(NY, y, lambda i: greet(at_y(i)))
    each(NX, dp, lambda i: greet(at_x(i)))

    vt[...] = jnp.zeros_like(vt)
    pl.semaphore_wait(bar, 1 + (NZ - 1) + (NY - 1) + (NX - 1))

    swaps = [
        remote(idxb.at[c], idxb.at[c], C_IDX, 0, 0, at_core()),
        remote(k_ref.at[:, their_cols], kp.at[c], C_K, 0, 0, at_core()),
        remote(v_ref.at[:, their_cols], vp.at[c], C_V, 0, 0, at_core()),
        remote(q_ref.at[:, their_cols], qp.at[c], C_Q, 0, 0, at_core()),
        remote(g_ref, gp.at[c], C_G, 0, 0, at_core()),
    ]
    swaps[1].start()
    swaps[2].start()
    local[0].wait()
    sub = lax.broadcasted_iota(jnp.int32, (MEM, SEG), 0)
    idx = jnp.zeros((MEM, SEG), jnp.int32)
    for m in range(MEM):
        idx = jnp.where(sub == m, idx_ref[m], idx)
    idxb[c] = idx
    swaps[0].start()
    swaps[3].start()
    swaps[4].start()
    local[1].wait()
    local[2].wait()
    for s in swaps[:3]:
        s.wait_recv()

    lane = lax.broadcasted_iota(jnp.int32, (MEM, SEG), 1)
    zero = jnp.zeros((MEM, SEG), F32)
    one_a = jnp.where(idxb[0] == lane, 1.0, 0.0).astype(F32)
    one_b = jnp.where(idxb[1] == lane, 1.0, 0.0).astype(F32)
    oh[...] = jnp.concatenate(
        [jnp.concatenate([one_a, zero], 1), jnp.concatenate([zero, one_b], 1)], 0
    ).astype(BF16)
    k_pair = kp[...].reshape(2 * SEG, HALF)
    v_pair = vp[...].reshape(2 * SEG, HALF)
    kbuf[y, blk(z)] = nn(oh[...], k_pair).astype(BF16)
    vbuf[y, blk(z)] = nn(oh[...], v_pair).astype(BF16)

    each(NZ, z, lambda i: remote(kbuf.at[y, blk(z)], kbuf.at[y, blk(z)], KZ, 0, 0, at_z(i)).start())
    span(0, NY - 1 - y, lambda i: remote(vbuf.at[y, blk(z)], vbuf.at[y, blk(z)], VY, NY - 1 - i, y, at_y(NY - 1 - i)).start())

    local[3].wait()
    swaps[3].wait_recv()
    lanes = lax.broadcasted_iota(jnp.int32, (2 * SEG, HALF), 1) // HEAD_DIM
    q_pair = (qp[...].reshape(2 * SEG, HALF).astype(F32) * (1.0 / math.sqrt(HEAD_DIM))).astype(BF16)
    for h in range(HEADS):
        q4[pl.ds(h * 256, 256), :] = jnp.where(lanes == h, q_pair, jnp.zeros_like(q_pair))

    def score_block(keys):
        return nt(keys, q4[...])

    col = lax.broadcasted_iota(jnp.int32, (2 * SEG, COLS), 1)
    row = lax.broadcasted_iota(jnp.int32, (2 * SEG, COLS), 0)
    s = score_block(k_pair)
    s = jnp.where((row // SEG) == ((col // SEG) % 2), s, -jnp.inf)
    s_loc[...] = s
    m8[...] = rows8(s, jnp.max)

    local[4].wait()
    local[5].wait()
    swaps[4].wait_recv()
    g_pair = gp[...].reshape(2 * SEG, D)
    ga = nt(g_pair, wh[...]).astype(BF16)
    gat[...] = nt(wh[...], g_pair).astype(BF16).astype(F32)
    for h in range(HEADS):
        ga4[pl.ds(h * 256, 256), :] = jnp.where(lanes == h, ga, jnp.zeros_like(ga))

    arrived(kbuf.at[y, pl.ds(0, 112)], KZ)

    up_y, dn_y, up_z, dn_z = (y + 1) % NY, (y + NY - 1) % NY, (z + 1) % NZ, (z + NZ - 1) % NZ

    def k_pass(phase, device, b, part, hops):
        ref = kbuf.at[b, pl.ds(part * (SEG // PARTS), SEG // PARTS)]
        at = hops * PARTS + part
        return remote(ref, ref, phase, at, at, device)

    def v_pass(phase, device, b, part, hops):
        ref = vbuf.at[pl.ds(part * (NY // PARTS), NY // PARTS), blk(b)]
        return remote(ref, ref, phase, 0, hops * PARTS + part, device)

    def k_up(b, part, hops):
        return k_pass(KU, at_y(up_y), b, part, hops)

    def k_dn(b, part, hops):
        return k_pass(KD, at_y(dn_y), b, part, hops)

    def v_up(b, part, hops):
        return v_pass(VU, at_z(up_z), b, part, hops)

    def v_dn(b, part, hops):
        return v_pass(VD, at_z(dn_z), b, part, hops)

    def begin(copy, b):
        for part in range(PARTS):
            copy(b, part, 0).start()

    def hand_on(copy, b, step, more):
        for part in range(PARTS):
            copy(b, part, step - 1).wait_recv()

            @pl.when(more)
            def _():
                copy(b, part, step).start()

    @pl.when(y < NY - 1)
    def _():
        begin(k_up, y)

    @pl.when(y <= 2)
    def _():
        begin(k_dn, y)

    span(0, y, lambda i: remote(vbuf.at[y, blk(z)], vbuf.at[i, blk(z)], VY, i, i, at_y(i)).wait_recv())
    begin(v_up, z)
    begin(v_dn, z)

    def masked(block):
        at = lax.broadcasted_iota(jnp.int32, (SEG, COLS), 0) // MEM
        seg = 2 * z + (lax.broadcasted_iota(jnp.int32, (SEG, COLS), 1) // SEG) % 2
        return jnp.where(at < seg, block, -jnp.inf)

    s = masked(score_block(kbuf[y]))
    s_mem[y] = s
    m8[...] = jnp.maximum(m8[...], rows8(s, jnp.max))

    def scores_of(i):
        block = score_block(kbuf[i])
        s_mem[i] = block
        m8[...] = jnp.maximum(m8[...], rows8(block, jnp.max))

    def gather_step(step):
        below, above = y - step, (y + step) % NY
        from_above = (step <= 3) & (above <= 2)

        @pl.when(below >= 0)
        def _():
            hand_on(k_up, below, step, (step < 4) & (y < NY - 1))

        @pl.when(from_above)
        def _():
            hand_on(k_dn, above, step, step < 3)

        @pl.when(step <= 3)
        def _():
            hand_on(v_up, (z + NZ - step) % NZ, step, step < 4)
            hand_on(v_dn, (z + step) % NZ, step, step < 3)

        @pl.when(below >= 0)
        def _():
            scores_of(below)

        @pl.when(from_above & (above < y))
        def _():
            scores_of(above)

    span(1, 5, gather_step)
    pairs = y // 2 + 1

    @pl.when(y % 2 == 0)
    def _():
        s_mem[y + 1] = jnp.full((SEG, COLS), -jnp.inf, F32)

    def two(i):
        return pl.ds(2 * i, 2)

    top = jnp.max(m8[...], axis=0, keepdims=True)

    def add_attended(values, p):
        p_low = p.astype(BF16)
        vals_t = values.T
        for h in range(HEADS):
            rows = pl.ds(h * HEAD_DIM, HEAD_DIM)
            acc[rows, :] = acc[rows, :] + nn(
                vals_t[h * HEAD_DIM : (h + 1) * HEAD_DIM], p_low[:, h * 256 : (h + 1) * 256]
            )

    p = jnp.exp(s_loc[...] - top)
    s_loc[...] = p
    l8[...] = rows8(p, jnp.sum)
    acc[...] = jnp.zeros_like(acc)
    add_attended(v_pair, p)

    def soft_of(i):
        p = jnp.exp(s_mem[two(i)].reshape(2 * SEG, COLS) - top)
        s_mem[two(i)] = p.reshape(2, SEG, COLS)
        l8[...] = l8[...] + rows8(p, jnp.sum)

    span(0, pairs, soft_of)

    for part in range(PARTS):
        v_up((z + NZ - 4) % NZ, part, 3).wait_recv()

    def attended_of(i):
        add_attended(vbuf[two(i)].reshape(2 * SEG, HALF), s_mem[two(i)].reshape(2 * SEG, COLS))

    span(0, pairs, attended_of)
    inv = 1.0 / jnp.sum(l8[...], axis=0, keepdims=True)
    att = jnp.concatenate(
        [acc[h * HEAD_DIM : (h + 1) * HEAD_DIM, :] * inv[:, h * 256 : (h + 1) * 256] for h in range(HEADS)], 0
    ).astype(BF16)
    term = nn(att, g_pair)
    wt[...] = term
    wsend[...] = term.astype(BF16)

    def wrows(i):
        return pl.ds(pl.multiple_of(i * 64, 64), 64)

    each(NX, dp, lambda i: remote(wsend.at[wrows(i)], wxr.at[dp], WX, 0, 0, at_x(i)).start())

    prod = att.astype(F32) * gat[...]
    delta = jnp.concatenate(
        [jnp.sum(prod[h * HEAD_DIM : (h + 1) * HEAD_DIM, :], axis=0, keepdims=True) for h in range(HEADS)], 1
    )

    def back(keys, values, p):
        pn = p * inv
        soft = nt(values, ga4[...])
        gs = (pn * (soft - delta)).astype(BF16)
        k_term = nn(gs, q4[...])
        v_term = nn(pn.astype(BF16), ga4[...])
        keys_t = keys.T
        for h in range(HEADS):
            rows = pl.ds(h * HEAD_DIM, HEAD_DIM)
            qacc[rows, :] = qacc[rows, :] + nn(
                keys_t[h * HEAD_DIM : (h + 1) * HEAD_DIM], gs[:, h * 256 : (h + 1) * 256]
            )
        return k_term, v_term

    qacc[...] = jnp.zeros_like(qacc)

    def back_of(i):
        k_term, v_term = back(
            kbuf[two(i)].reshape(2 * SEG, HALF), vbuf[two(i)].reshape(2 * SEG, HALF),
            s_mem[two(i)].reshape(2 * SEG, COLS),
        )
        kt[two(i)] = k_term.astype(BF16).reshape(2, SEG, HALF)
        vt[two(i)] = v_term.astype(BF16).reshape(2, SEG, HALF)
        for j in (2 * i, 2 * i + 1):
            @pl.when(j < y)
            def _():
                remote(kt.at[j], kry.at[y], RKY, j, y, at_y(j)).start()

        @pl.when(i == 1)
        def _():
            v_half(0)

    def v_send(half, i):
        part = pl.ds(half * 4, 4)
        return remote(vt.at[part, blk(i)], vrz.at[z, part], RVZ + half, 0, 0, at_z(i))

    def v_half(half):
        each(NZ, z, lambda i: v_send(half, i).start())

    span(0, pairs, back_of)

    @pl.when(y < 2)
    def _():
        v_half(0)

    @pl.when(y >= 4)
    def _():
        v_half(1)

    k_term, v_term = back(k_pair, v_pair, s_loc[...])
    kg[...] = k_term
    vg[...] = v_term
    qg = (qacc[...] * (1.0 / math.sqrt(HEAD_DIM))).T.astype(BF16)
    obq[...] = qg.reshape(2, SEG, HALF)
    out_q = remote(obq.at[other], qo_ref.at[:, my_cols], O_Q, 0, 0, at_core())
    out_q.start()
    keep_q = pltpu.make_async_copy(obq.at[c], qo_ref.at[:, my_cols], lsem.at[6])
    keep_q.start()

    for s in swaps:
        s.wait_send()
    left(kbuf.at[y, pl.ds(0, 112)], KZ)
    span(y + 1, NY, lambda i: remote(vbuf.at[y, blk(z)], vbuf.at[y, blk(z)], VY, i, y, at_y(i)).wait_send())

    def sent(copy, b, step):
        for part in range(PARTS):
            copy(b, part, step).wait_send()

    def gather_sent(step):
        below, above = y - step, (y + step) % NY

        @pl.when((below >= 0) & (y < NY - 1))
        def _():
            sent(k_up, below, step)

        @pl.when((step < 3) & (above <= 2))
        def _():
            sent(k_dn, above, step)

    span(0, 4, gather_sent)
    left(vbuf.at[:, pl.ds(0, 64)], VU)
    left(vbuf.at[:, pl.ds(0, 48)], VD)

    arrived(wxr.at[pl.ds(0, NX - 1)], WX)

    def add_x(i):
        wt[wrows(dp), :] = wt[wrows(dp), :] + wxr[i].astype(F32)

    each(NX, dp, add_x, near=True)
    wxs[...] = wt[wrows(dp), :].astype(BF16)

    def wcols(i):
        return pl.ds(pl.multiple_of(i * 128, 128), 128)

    each(NY, y, lambda i: remote(wxs.at[:, wcols(i)], wyr.at[y], WY, 0, 0, at_y(i)).start())
    left(wsend.at[pl.ds(0, 192)], WX)

    def add_vz(half):
        part = pl.ds(half * 4, 4)
        arrived(vrz.at[pl.ds(0, NZ - 1), part], RVZ + half)
        left(vt.at[part, pl.ds(0, 112)], RVZ + half)
        vsum[part] = vt[part, blk(z)].astype(F32)

        def add(i):
            vsum[part] = vsum[part] + vrz[i, part].astype(F32)

        each(NZ, z, add, near=True)

    add_vz(0)

    @pl.when(y >= 4)
    def _():
        add_vz(1)

    vrow[...] = vsum[...].astype(BF16)
    span(0, y, lambda i: remote(vrow.at[i], vry.at[y], RVY, i, y, at_y(i)).start())

    wys[...] = wt[wrows(dp), wcols(y)]

    arrived(wyr.at[pl.ds(0, NY - 1)], WY)

    def add_y(i):
        wys[...] = wys[...] + wyr[i].astype(F32)

    each(NY, y, add_y, near=True)
    wzr[z] = wys[...].astype(BF16)
    each(NZ, z, lambda i: remote(wzr.at[z], wzr.at[z], WZ, 0, 0, at_z(i)).start())
    left(wxs.at[:, pl.ds(0, 896)], WY)
    span(0, y, lambda i: remote(kt.at[i], kry.at[y], RKY, i, y, at_y(i)).wait_send())

    ksum[...] = kt[y].astype(F32)

    def add_ky(i):
        remote(kt.at[0], kry.at[i], RKY, 0, i, at_y(i)).wait_recv()
        ksum[...] = ksum[...] + kry[i].astype(F32)

    span(y + 1, NY, add_ky)
    krow[...] = ksum[...].astype(BF16)
    each(NZ, z, lambda i: remote(krow.at[blk(i)], krz.at[z], RKZ, 0, 0, at_z(i)).start())

    arrived(wzr.at[pl.ds(0, NZ - 1)], WZ)
    total = wzr[0].astype(F32)
    for i in range(1, NZ):
        total = total + wzr[i].astype(F32)

    def piece(i, j):
        return wo_ref.at[wrows(i), wcols(j)]

    def out_rows(half, i):
        return wout_ref.at[pl.ds(pl.multiple_of(half * HALF + i * 64, 64), 64)]

    def out_piece(half, i, j):
        return wout_ref.at[pl.ds(pl.multiple_of(half * HALF + i * 64, 64), 64), wcols(j)]

    wo_ref[wrows(dp), wcols(y)] = (total * (1.0 / math.sqrt(4 * 16384))).astype(BF16)
    here = piece(dp, y)

    def send_x(i, j, at):
        return remote(piece(dp, j), piece(dp, j), GX, i, at, at_x(i))

    x_up, x_dn, across = (dp + 1) % NX, (dp + 3) % NX, (dp + 2) % NX

    def nth(n):
        return (y + (1 - 2 * (n % 2)) * ((n + 1) // 2)) % NY

    def to_x(n):
        j = nth(n)
        send_x(x_up, j, FROM_LEFT).start()
        send_x(x_dn, j, FROM_RIGHT + n - n // 4 * (n - 4)).start()

        @pl.when(n >= 4)
        def _():
            send_x(across, j, FROM_ACROSS).start()

        remote(piece(dp, j), out_piece(c, dp, j), GC, 0, 0, at_core()).start()

    mine = wo_ref.at[wrows(dp)]

    def keep(i):
        return pltpu.make_async_copy(wo_ref.at[wrows(i)], out_rows(c, i), lsem.at[9])

    each(NY, y, lambda i: remote(here, here, GY, 0, y, at_y(i)).start())
    to_x(0)

    def from_y(n):
        i = nth(n)
        remote(here, piece(dp, i), GY, i, i, at_y(i)).wait_recv()
        to_x(n)

    span(1, NY, from_y)

    def pass_on(n):
        ref = piece(x_up, nth(n))
        arrived(ref, GX, FROM_RIGHT + n)
        pltpu.make_async_remote_copy(
            src_ref=ref, dst_ref=ref, send_sem=ssem.at[SENDS[GR]], recv_sem=rsem.at[ARRIVALS[GX] + FROM_ACROSS],
            device_id=at_x(x_dn), device_id_type=MESH,
        ).start()

    span(0, 4, pass_on)
    keep(dp).start()

    vsum_own[...] = vsum[y]

    def add_vy(i):
        remote(vrow.at[0], vry.at[i], RVY, 0, i, at_y(i)).wait_recv()
        vsum_own[...] = vsum_own[...] + vry[i].astype(F32)

    span(y + 1, NY, add_vy)
    kown = ksum.at[blk(z)]

    arrived(krz.at[pl.ds(0, NZ - 1)], RKZ)

    def add_kz(i):
        kown[...] = kown[...] + krz[i].astype(F32)

    each(NZ, z, add_kz, near=True)

    def place(local, terms):
        hi = terms.astype(BF16)
        lo = (terms - hi.astype(F32)).astype(BF16)
        return (local + (tn(oh[...], hi) + tn(oh[...], lo))).astype(BF16).reshape(2, SEG, HALF)

    obk[...] = place(kg[...], kown[...])
    obv[...] = place(vg[...], vsum_own[...])
    out_k = remote(obk.at[other], ko_ref.at[:, my_cols], O_K, 0, 0, at_core())
    out_v = remote(obv.at[other], vo_ref.at[:, my_cols], O_V, 0, 0, at_core())
    out_k.start()
    out_v.start()
    keep_k = pltpu.make_async_copy(obk.at[c], ko_ref.at[:, my_cols], lsem.at[7])
    keep_v = pltpu.make_async_copy(obv.at[c], vo_ref.at[:, my_cols], lsem.at[8])
    keep_k.start()
    keep_v.start()

    left(krow.at[pl.ds(0, 112)], RKZ)
    span(0, y, lambda i: remote(vrow.at[i], vry.at[y], RVY, i, y, at_y(i)).wait_send())
    left(wzr.at[pl.ds(0, NZ - 1)], WZ)
    out_q.wait()
    out_k.wait()
    out_v.wait()

    def from_x(i, first, at):
        arrived(wo_ref.at[wrows(i), pl.ds(0, (NY - first) * 128)], GX, at)
        remote(wo_ref.at[wrows(i)], out_rows(c, i), GD, 0, 0, at_core()).start()
        keep(i).start()

    from_x(x_up, 4, FROM_RIGHT + 4)
    from_x(x_dn, 0, FROM_LEFT)
    from_x(across, 0, FROM_ACROSS)
    arrived(out_rows(other, dp), GC)
    arrived(wout_ref.at[pl.ds(0, 192)], GD)
    pltpu.make_async_copy(wo_ref, wout_ref.at[pl.ds(0, HALF)], lsem.at[9]).wait()
    keep_q.wait()
    keep_k.wait()
    keep_v.wait()

    left(wo_ref.at[pl.ds(0, 64), pl.ds(0, 896)], GY)
    left(mine, GC)
    left(mine, GX, x_up)
    left(mine, GX, x_dn)
    left(wo_ref.at[wrows(dp), pl.ds(0, D // 2)], GX, across)
    left(wo_ref.at[pl.ds(0, 64), pl.ds(0, D // 2)], GR)
    left(wo_ref.at[pl.ds(0, 192)], GD)


def store(*refs):
    arrays, outs, held, sem = refs[:4], refs[4:8], refs[8:12], refs[12]
    loads = [pltpu.make_async_copy(arrays[i], held[i], sem.at[0, i]) for i in range(4)]
    stores = [pltpu.make_async_copy(held[i], outs[i], sem.at[1, i]) for i in range(4)]
    for copy in loads:
        copy.start()
    for load, copy in zip(loads, stores):
        load.wait()
        copy.start()
    for copy in stores:
        copy.wait()


def on_device(query_rows, key_rows, value_rows, out_grad, out_weight, memory_index):
    V = pltpu.VMEM
    scratch = [
        pltpu.SMEM((MEM,), jnp.int32), V((2, MEM, SEG), jnp.int32),
        V((2, SEG, HALF), BF16), V((2, SEG, HALF), BF16), V((2, SEG, HALF), BF16),
        V((2, SEG, D), BF16), V((HALF, D), BF16),
        V((COLS, HALF), BF16), V((COLS, HALF), BF16), V((HALF, HALF), F32),
        V((16, HALF), BF16),
        V((NY, SEG, HALF), BF16), V((NY, SEG, HALF), BF16),
        V((NY, SEG, COLS), F32), V((2 * SEG, COLS), F32),
        V((8, COLS), F32), V((8, COLS), F32),
        V((HALF, HALF), F32), V((HALF, HALF), F32),
        V((NY, SEG, HALF), BF16), V((NY, SEG, HALF), BF16),
        V((HALF, HALF), F32), V((HALF, HALF), F32),
        V((NY, SEG, HALF), BF16), V((NZ, 16, HALF), BF16),
        V((NZ, NY, 16, HALF), BF16), V((NY, 16, HALF), BF16),
        V((SEG, HALF), F32), V((NY, 16, HALF), F32), V((16, HALF), F32),
        V((SEG, HALF), BF16), V((NY, 16, HALF), BF16),
        V((HALF, D), F32), V((HALF, D), BF16),
        V((NX, 64, D), BF16), V((64, D), BF16),
        V((NY, 64, 128), BF16), V((64, 128), F32),
        V((NZ, 64, 128), BF16), V((HALF, D), BF16),
        V((2, SEG, HALF), BF16), V((2, SEG, HALF), BF16), V((2, SEG, HALF), BF16),
        pltpu.SemaphoreType.DMA((SENDS[-1],)), pltpu.SemaphoreType.DMA((ARRIVALS[-1],)), pltpu.SemaphoreType.DMA((10,)),
    ]
    qg, kgrad, vgrad, wgrad = pl.pallas_call(
        kernel,
        out_shape=(
            jax.ShapeDtypeStruct((SEG, HD), BF16),
            jax.ShapeDtypeStruct((SEG, HD), BF16),
            jax.ShapeDtypeStruct((SEG, HD), BF16),
            jax.ShapeDtypeStruct((HD, D), BF16),
        ),
        in_specs=[pl.BlockSpec(memory_space=pltpu.HBM)] * 6,
        out_specs=[pl.BlockSpec(memory_space=pltpu.HBM)] * 4,
        scratch_shapes=scratch,
        compiler_params=pltpu.CompilerParams(
            collective_id=0, has_side_effects=True, vmem_limit_bytes=64 * 2**20
        ),
        name="memory_attention_backward",
    )(memory_index[0], query_rows[0], key_rows[0], value_rows[0], out_grad[0], out_weight)
    qg, kgrad, vgrad, wgrad = pl.pallas_call(
        store,
        out_shape=tuple(jax.ShapeDtypeStruct(a.shape, a.dtype) for a in (qg, kgrad, vgrad, wgrad)),
        in_specs=[pl.BlockSpec(memory_space=pltpu.HBM)] * 4,
        compiler_params=pltpu.CompilerParams(vmem_limit_bytes=64 * 2**20),
        out_specs=[pl.BlockSpec(memory_space=pltpu.HBM)] * 4,
        scratch_shapes=[V((SEG, HD), BF16)] * 3 + [V((HD, D), BF16), pltpu.SemaphoreType.DMA((2, 4))],
        name="store_results",
    )(qg, kgrad, vgrad, wgrad)
    return qg[None], kgrad[None], vgrad[None], wgrad


def solution(mesh):
    placed = (
        P("dp", "tm", None),
        P("dp", "tm", None),
        P("dp", "tm", None),
        P("dp", "tm", None),
        P(),
        P("dp", "tm", None),
    )
    return jax.shard_map(
        on_device,
        mesh=mesh,
        in_specs=placed,
        out_specs=(P("dp", "tm", None), P("dp", "tm", None), P("dp", "tm", None), P()),
        check_vma=False,
    )
```

```python
import math

import jax
import jax.numpy as jnp
from jax import lax
from jax.experimental import pallas as pl
from jax.experimental.pallas import tpu as pltpu
from jax.sharding import PartitionSpec as P

HEAD_DIM = 64
SEG = 128
MEM = 8
HD = 512
D = 1024
HALF = 256
HEADS = 4
COLS = HEADS * 2 * SEG
NY, NZ, NX = 8, 8, 4
MESH = pl.DeviceIdType.MESH
F32, BF16 = jnp.float32, jnp.bfloat16

PARTS = 2
(
    C_IDX, C_K, C_V, C_Q, C_G, KZ, KU, KD, VY, VU, VD, RKY, RKZ, RVZ, RVZ1, RVY,
    WX, WY, WZ, GY, GX, GR, GC, GD, O_Q, O_K, O_V,
) = range(27)
COUNTS = [(1, 1)] * 27
COUNTS[KU], COUNTS[KD], COUNTS[VU], COUNTS[VD] = (4 * PARTS,) * 2, (3 * PARTS,) * 2, (1, 4 * PARTS), (1, 3 * PARTS)
COUNTS[VY] = COUNTS[RKY] = COUNTS[RVY] = (NY, NY)
COUNTS[GY], COUNTS[GX] = (1, NY), (NX, 7)
SENDS = [sum(n for n, _ in COUNTS[:i]) for i in range(28)]
ARRIVALS = [sum(n for _, n in COUNTS[:i]) for i in range(28)]
FROM_RIGHT, FROM_LEFT, FROM_ACROSS = 0, 5, 6


def nt(a, b):
    return lax.dot_general(a, b, (((1,), (1,)), ((), ())), preferred_element_type=F32)


def tn(a, b):
    return lax.dot_general(a, b, (((0,), (0,)), ((), ())), preferred_element_type=F32)


def nn(a, b):
    return jnp.dot(a, b, preferred_element_type=F32)


def rows8(block, op):
    return op(block.reshape(block.shape[0] // 8, 8, block.shape[1]), axis=0)


def kernel(
    idx_in, q_ref, k_ref, v_ref, g_ref, w_ref,
    qo_ref, ko_ref, vo_ref, wout_ref,
    idx_ref, idxb, kp, vp, qp, gp, wh, q4, ga4, gat, oh, kbuf, vbuf, s_mem, s_loc,
    m8, l8, acc, qacc, kt, vt, kg, vg, kry, krz, vrz, vry, ksum, vsum, vsum_own, krow, vrow,
    wt, wsend, wxr, wxs, wyr, wys, wzr, wo_ref, obq, obk, obv,
    ssem, rsem, lsem,
):
    dp, tm = lax.axis_index("dp"), lax.axis_index("tm")
    c, z, y = tm % 2, (tm // 2) % NZ, tm // (2 * NZ)
    other = 1 - c

    def at_core():
        return (dp, y * 16 + z * 2 + other)

    def at_z(i):
        return (dp, y * 16 + i * 2 + c)

    def at_y(i):
        return (dp, i * 16 + z * 2 + c)

    def at_x(i):
        return (i, tm)

    def remote(src, dst, phase, mine, theirs, device):
        return pltpu.make_async_remote_copy(
            src_ref=src, dst_ref=dst, send_sem=ssem.at[SENDS[phase] + mine],
            recv_sem=rsem.at[ARRIVALS[phase] + theirs],
            device_id=device, device_id_type=MESH,
        )

    def far(count, k):
        return count // 2 + (1 - 2 * (k % 2)) * ((k + 1) // 2)

    def arrived(ref, phase, at=0):
        remote(ref, ref, phase, 0, at, at_core()).wait_recv()

    def left(ref, phase, at=0):
        remote(ref, ref, phase, at, 0, at_core()).wait_send()

    def each(count, me, body, near=False):
        def step(k, _):
            body((me + far(count, count - 2 - k if near else k)) % count)
            return 0

        lax.fori_loop(0, count - 1, step, 0)

    def span(lo, hi, body):
        def step(i, _):
            body(i)
            return 0

        lax.fori_loop(lo, hi, step, 0)

    def blk(i):
        return pl.ds(pl.multiple_of(i * 16, 16), 16)

    my_cols = pl.ds(pl.multiple_of(c * HALF, HALF), HALF)
    their_cols = pl.ds(pl.multiple_of(other * HALF, HALF), HALF)

    kbuf[...] = jnp.zeros_like(kbuf)
    vbuf[...] = jnp.zeros_like(vbuf)

    local = [
        pltpu.make_async_copy(src, dst, lsem.at[i])
        for i, (src, dst) in enumerate((
            (idx_in.at[0], idx_ref),
            (k_ref.at[:, my_cols], kp.at[c]),
            (v_ref.at[:, my_cols], vp.at[c]),
            (q_ref.at[:, my_cols], qp.at[c]),
            (g_ref, gp.at[c]),
            (w_ref.at[pl.ds(pl.multiple_of(c * HALF, HALF), HALF)], wh),
        ))
    ]
    for copy in local:
        copy.start()

    bar = pltpu.get_barrier_semaphore()

    def greet(device):
        pl.semaphore_signal(bar, inc=1, device_id=device, device_id_type=MESH)

    greet(at_core())
    each(NZ, z, lambda i: greet(at_z(i)))
    each(NY, y, lambda i: greet(at_y(i)))
    each(NX, dp, lambda i: greet(at_x(i)))

    vt[...] = jnp.zeros_like(vt)
    pl.semaphore_wait(bar, 1 + (NZ - 1) + (NY - 1) + (NX - 1))

    swaps = [
        remote(idxb.at[c], idxb.at[c], C_IDX, 0, 0, at_core()),
        remote(k_ref.at[:, their_cols], kp.at[c], C_K, 0, 0, at_core()),
        remote(v_ref.at[:, their_cols], vp.at[c], C_V, 0, 0, at_core()),
        remote(q_ref.at[:, their_cols], qp.at[c], C_Q, 0, 0, at_core()),
        remote(g_ref, gp.at[c], C_G, 0, 0, at_core()),
    ]
    swaps[1].start()
    swaps[2].start()
    local[0].wait()
    sub = lax.broadcasted_iota(jnp.int32, (MEM, SEG), 0)
    idx = jnp.zeros((MEM, SEG), jnp.int32)
    for m in range(MEM):
        idx = jnp.where(sub == m, idx_ref[m], idx)
    idxb[c] = idx
    swaps[0].start()
    swaps[3].start()
    swaps[4].start()
    local[1].wait()
    local[2].wait()
    for s in swaps[:3]:
        s.wait_recv()

    lane = lax.broadcasted_iota(jnp.int32, (MEM, SEG), 1)
    zero = jnp.zeros((MEM, SEG), F32)
    one_a = jnp.where(idxb[0] == lane, 1.0, 0.0).astype(F32)
    one_b = jnp.where(idxb[1] == lane, 1.0, 0.0).astype(F32)
    oh[...] = jnp.concatenate(
        [jnp.concatenate([one_a, zero], 1), jnp.concatenate([zero, one_b], 1)], 0
    ).astype(BF16)
    k_pair = kp[...].reshape(2 * SEG, HALF)
    v_pair = vp[...].reshape(2 * SEG, HALF)
    kbuf[y, blk(z)] = nn(oh[...], k_pair).astype(BF16)
    vbuf[y, blk(z)] = nn(oh[...], v_pair).astype(BF16)

    each(NZ, z, lambda i: remote(kbuf.at[y, blk(z)], kbuf.at[y, blk(z)], KZ, 0, 0, at_z(i)).start())
    span(0, NY - 1 - y, lambda i: remote(vbuf.at[y, blk(z)], vbuf.at[y, blk(z)], VY, NY - 1 - i, y, at_y(NY - 1 - i)).start())

    local[3].wait()
    swaps[3].wait_recv()
    lanes = lax.broadcasted_iota(jnp.int32, (2 * SEG, HALF), 1) // HEAD_DIM
    q_pair = (qp[...].reshape(2 * SEG, HALF).astype(F32) * (1.0 / math.sqrt(HEAD_DIM))).astype(BF16)
    for h in range(HEADS):
        q4[pl.ds(h * 256, 256), :] = jnp.where(lanes == h, q_pair, jnp.zeros_like(q_pair))

    def score_block(keys):
        return nt(keys, q4[...])

    col = lax.broadcasted_iota(jnp.int32, (2 * SEG, COLS), 1)
    row = lax.broadcasted_iota(jnp.int32, (2 * SEG, COLS), 0)
    s = score_block(k_pair)
    s = jnp.where((row // SEG) == ((col // SEG) % 2), s, -jnp.inf)
    s_loc[...] = s
    m8[...] = rows8(s, jnp.max)

    local[4].wait()
    local[5].wait()
    swaps[4].wait_recv()
    g_pair = gp[...].reshape(2 * SEG, D)
    ga = nt(g_pair, wh[...]).astype(BF16)
    gat[...] = nt(wh[...], g_pair).astype(BF16).astype(F32)
    for h in range(HEADS):
        ga4[pl.ds(h * 256, 256), :] = jnp.where(lanes == h, ga, jnp.zeros_like(ga))

    arrived(kbuf.at[y, pl.ds(0, 112)], KZ)

    up_y, dn_y, up_z, dn_z = (y + 1) % NY, (y + NY - 1) % NY, (z + 1) % NZ, (z + NZ - 1) % NZ

    def k_pass(phase, device, b, part, hops):
        ref = kbuf.at[b, pl.ds(part * (SEG // PARTS), SEG // PARTS)]
        at = hops * PARTS + part
        return remote(ref, ref, phase, at, at, device)

    def v_pass(phase, device, b, part, hops):
        ref = vbuf.at[pl.ds(part * (NY // PARTS), NY // PARTS), blk(b)]
        return remote(ref, ref, phase, 0, hops * PARTS + part, device)

    def k_up(b, part, hops):
        return k_pass(KU, at_y(up_y), b, part, hops)

    def k_dn(b, part, hops):
        return k_pass(KD, at_y(dn_y), b, part, hops)

    def v_up(b, part, hops):
        return v_pass(VU, at_z(up_z), b, part, hops)

    def v_dn(b, part, hops):
        return v_pass(VD, at_z(dn_z), b, part, hops)

    def begin(copy, b):
        for part in range(PARTS):
            copy(b, part, 0).start()

    def hand_on(copy, b, step, more):
        for part in range(PARTS):
            copy(b, part, step - 1).wait_recv()

            @pl.when(more)
            def _():
                copy(b, part, step).start()

    @pl.when(y < NY - 1)
    def _():
        begin(k_up, y)

    @pl.when(y <= 2)
    def _():
        begin(k_dn, y)

    span(0, y, lambda i: remote(vbuf.at[y, blk(z)], vbuf.at[i, blk(z)], VY, i, i, at_y(i)).wait_recv())
    begin(v_up, z)
    begin(v_dn, z)

    def masked(block):
        at = lax.broadcasted_iota(jnp.int32, (SEG, COLS), 0) // MEM
        seg = 2 * z + (lax.broadcasted_iota(jnp.int32, (SEG, COLS), 1) // SEG) % 2
        return jnp.where(at < seg, block, -jnp.inf)

    s = masked(score_block(kbuf[y]))
    s_mem[y] = s
    m8[...] = jnp.maximum(m8[...], rows8(s, jnp.max))

    def scores_of(i):
        block = score_block(kbuf[i])
        s_mem[i] = block
        m8[...] = jnp.maximum(m8[...], rows8(block, jnp.max))

    def gather_step(step):
        below, above = y - step, (y + step) % NY
        from_above = (step <= 3) & (above <= 2)

        @pl.when(below >= 0)
        def _():
            hand_on(k_up, below, step, (step < 4) & (y < NY - 1))

        @pl.when(from_above)
        def _():
            hand_on(k_dn, above, step, step < 3)

        @pl.when(step <= 3)
        def _():
            hand_on(v_up, (z + NZ - step) % NZ, step, step < 4)
            hand_on(v_dn, (z + step) % NZ, step, step < 3)

        @pl.when(below >= 0)
        def _():
            scores_of(below)

        @pl.when(from_above & (above < y))
        def _():
            scores_of(above)

    span(1, 5, gather_step)
    pairs = y // 2 + 1

    @pl.when(y % 2 == 0)
    def _():
        s_mem[y + 1] = jnp.full((SEG, COLS), -jnp.inf, F32)

    def two(i):
        return pl.ds(2 * i, 2)

    top = jnp.max(m8[...], axis=0, keepdims=True)

    def add_attended(values, p):
        p_low = p.astype(BF16)
        vals_t = values.T
        for h in range(HEADS):
            rows = pl.ds(h * HEAD_DIM, HEAD_DIM)
            acc[rows, :] = acc[rows, :] + nn(
                vals_t[h * HEAD_DIM : (h + 1) * HEAD_DIM], p_low[:, h * 256 : (h + 1) * 256]
            )

    p = jnp.exp(s_loc[...] - top)
    s_loc[...] = p
    l8[...] = rows8(p, jnp.sum)
    acc[...] = jnp.zeros_like(acc)
    add_attended(v_pair, p)

    def soft_of(i):
        p = jnp.exp(s_mem[two(i)].reshape(2 * SEG, COLS) - top)
        s_mem[two(i)] = p.reshape(2, SEG, COLS)
        l8[...] = l8[...] + rows8(p, jnp.sum)

    span(0, pairs, soft_of)

    for part in range(PARTS):
        v_up((z + NZ - 4) % NZ, part, 3).wait_recv()

    def attended_of(i):
        add_attended(vbuf[two(i)].reshape(2 * SEG, HALF), s_mem[two(i)].reshape(2 * SEG, COLS))

    span(0, pairs, attended_of)
    inv = 1.0 / jnp.sum(l8[...], axis=0, keepdims=True)
    att = jnp.concatenate(
        [acc[h * HEAD_DIM : (h + 1) * HEAD_DIM, :] * inv[:, h * 256 : (h + 1) * 256] for h in range(HEADS)], 0
    ).astype(BF16)
    term = nn(att, g_pair)
    wt[...] = term
    wsend[...] = term.astype(BF16)

    def wrows(i):
        return pl.ds(pl.multiple_of(i * 64, 64), 64)

    each(NX, dp, lambda i: remote(wsend.at[wrows(i)], wxr.at[dp], WX, 0, 0, at_x(i)).start())

    prod = att.astype(F32) * gat[...]
    delta = jnp.concatenate(
        [jnp.sum(prod[h * HEAD_DIM : (h + 1) * HEAD_DIM, :], axis=0, keepdims=True) for h in range(HEADS)], 1
    )

    def back(keys, values, p):
        pn = p * inv
        soft = nt(values, ga4[...])
        gs = (pn * (soft - delta)).astype(BF16)
        k_term = nn(gs, q4[...])
        v_term = nn(pn.astype(BF16), ga4[...])
        keys_t = keys.T
        for h in range(HEADS):
            rows = pl.ds(h * HEAD_DIM, HEAD_DIM)
            qacc[rows, :] = qacc[rows, :] + nn(
                keys_t[h * HEAD_DIM : (h + 1) * HEAD_DIM], gs[:, h * 256 : (h + 1) * 256]
            )
        return k_term, v_term

    qacc[...] = jnp.zeros_like(qacc)

    def back_of(i):
        k_term, v_term = back(
            kbuf[two(i)].reshape(2 * SEG, HALF), vbuf[two(i)].reshape(2 * SEG, HALF),
            s_mem[two(i)].reshape(2 * SEG, COLS),
        )
        kt[two(i)] = k_term.astype(BF16).reshape(2, SEG, HALF)
        vt[two(i)] = v_term.astype(BF16).reshape(2, SEG, HALF)
        for j in (2 * i, 2 * i + 1):
            @pl.when(j < y)
            def _():
                remote(kt.at[j], kry.at[y], RKY, j, y, at_y(j)).start()

        @pl.when(i == 1)
        def _():
            v_half(0)

    def v_send(half, i):
        part = pl.ds(half * 4, 4)
        return remote(vt.at[part, blk(i)], vrz.at[z, part], RVZ + half, 0, 0, at_z(i))

    def v_half(half):
        each(NZ, z, lambda i: v_send(half, i).start())

    span(0, pairs, back_of)

    @pl.when(y < 2)
    def _():
        v_half(0)

    @pl.when(y >= 4)
    def _():
        v_half(1)

    k_term, v_term = back(k_pair, v_pair, s_loc[...])
    kg[...] = k_term
    vg[...] = v_term
    qg = (qacc[...] * (1.0 / math.sqrt(HEAD_DIM))).T.astype(BF16)
    obq[...] = qg.reshape(2, SEG, HALF)
    out_q = remote(obq.at[other], qo_ref.at[:, my_cols], O_Q, 0, 0, at_core())
    out_q.start()
    keep_q = pltpu.make_async_copy(obq.at[c], qo_ref.at[:, my_cols], lsem.at[6])
    keep_q.start()

    for s in swaps:
        s.wait_send()
    left(kbuf.at[y, pl.ds(0, 112)], KZ)
    span(y + 1, NY, lambda i: remote(vbuf.at[y, blk(z)], vbuf.at[y, blk(z)], VY, i, y, at_y(i)).wait_send())

    def sent(copy, b, step):
        for part in range(PARTS):
            copy(b, part, step).wait_send()

    def gather_sent(step):
        below, above = y - step, (y + step) % NY

        @pl.when((below >= 0) & (y < NY - 1))
        def _():
            sent(k_up, below, step)

        @pl.when((step < 3) & (above <= 2))
        def _():
            sent(k_dn, above, step)

    span(0, 4, gather_sent)
    left(vbuf.at[:, pl.ds(0, 64)], VU)
    left(vbuf.at[:, pl.ds(0, 48)], VD)

    arrived(wxr.at[pl.ds(0, NX - 1)], WX)

    def add_x(i):
        wt[wrows(dp), :] = wt[wrows(dp), :] + wxr[i].astype(F32)

    each(NX, dp, add_x, near=True)
    wxs[...] = wt[wrows(dp), :].astype(BF16)

    def wcols(i):
        return pl.ds(pl.multiple_of(i * 128, 128), 128)

    each(NY, y, lambda i: remote(wxs.at[:, wcols(i)], wyr.at[y], WY, 0, 0, at_y(i)).start())
    left(wsend.at[pl.ds(0, 192)], WX)

    wys[...] = wt[wrows(dp), wcols(y)]

    arrived(wyr.at[pl.ds(0, NY - 1)], WY)

    def add_y(i):
        wys[...] = wys[...] + wyr[i].astype(F32)

    each(NY, y, add_y, near=True)
    wzr[z] = wys[...].astype(BF16)
    each(NZ, z, lambda i: remote(wzr.at[z], wzr.at[z], WZ, 0, 0, at_z(i)).start())
    left(wxs.at[:, pl.ds(0, 896)], WY)
    span(0, y, lambda i: remote(kt.at[i], kry.at[y], RKY, i, y, at_y(i)).wait_send())

    ksum[...] = kt[y].astype(F32)

    def add_ky(i):
        remote(kt.at[0], kry.at[i], RKY, 0, i, at_y(i)).wait_recv()
        ksum[...] = ksum[...] + kry[i].astype(F32)

    span(y + 1, NY, add_ky)
    krow[...] = ksum[...].astype(BF16)
    each(NZ, z, lambda i: remote(krow.at[blk(i)], krz.at[z], RKZ, 0, 0, at_z(i)).start())

    def add_vz(half):
        part = pl.ds(half * 4, 4)
        arrived(vrz.at[pl.ds(0, NZ - 1), part], RVZ + half)
        left(vt.at[part, pl.ds(0, 112)], RVZ + half)
        vsum[part] = vt[part, blk(z)].astype(F32)

        def add(i):
            vsum[part] = vsum[part] + vrz[i, part].astype(F32)

        each(NZ, z, add, near=True)

    add_vz(0)

    @pl.when(y >= 4)
    def _():
        add_vz(1)

    vrow[...] = vsum[...].astype(BF16)
    span(0, y, lambda i: remote(vrow.at[i], vry.at[y], RVY, i, y, at_y(i)).start())

    arrived(wzr.at[pl.ds(0, NZ - 1)], WZ)
    total = wzr[0].astype(F32)
    for i in range(1, NZ):
        total = total + wzr[i].astype(F32)

    def piece(i, j):
        return wo_ref.at[wrows(i), wcols(j)]

    def out_rows(half, i):
        return wout_ref.at[pl.ds(pl.multiple_of(half * HALF + i * 64, 64), 64)]

    def out_piece(half, i, j):
        return wout_ref.at[pl.ds(pl.multiple_of(half * HALF + i * 64, 64), 64), wcols(j)]

    wo_ref[wrows(dp), wcols(y)] = (total * (1.0 / math.sqrt(4 * 16384))).astype(BF16)
    here = piece(dp, y)

    def send_x(i, j, at):
        return remote(piece(dp, j), piece(dp, j), GX, i, at, at_x(i))

    x_up, x_dn, across = (dp + 1) % NX, (dp + 3) % NX, (dp + 2) % NX

    def nth(n):
        return (y + (1 - 2 * (n % 2)) * ((n + 1) // 2)) % NY

    def to_x(n):
        j = nth(n)
        send_x(x_up, j, FROM_LEFT).start()
        send_x(x_dn, j, FROM_RIGHT + n - n // 4 * (n - 4)).start()

        @pl.when(n >= 4)
        def _():
            send_x(across, j, FROM_ACROSS).start()

        remote(piece(dp, j), out_piece(c, dp, j), GC, 0, 0, at_core()).start()

    mine = wo_ref.at[wrows(dp)]

    def keep(i):
        return pltpu.make_async_copy(wo_ref.at[wrows(i)], out_rows(c, i), lsem.at[9])

    each(NY, y, lambda i: remote(here, here, GY, 0, y, at_y(i)).start())
    to_x(0)

    vsum_own[...] = vsum[y]

    def add_vy(i):
        remote(vrow.at[0], vry.at[i], RVY, 0, i, at_y(i)).wait_recv()
        vsum_own[...] = vsum_own[...] + vry[i].astype(F32)

    span(y + 1, NY, add_vy)
    kown = ksum.at[blk(z)]

    arrived(krz.at[pl.ds(0, NZ - 1)], RKZ)

    def add_kz(i):
        kown[...] = kown[...] + krz[i].astype(F32)

    each(NZ, z, add_kz, near=True)

    def place(local, terms):
        hi = terms.astype(BF16)
        lo = (terms - hi.astype(F32)).astype(BF16)
        return (local + (tn(oh[...], hi) + tn(oh[...], lo))).astype(BF16).reshape(2, SEG, HALF)

    obk[...] = place(kg[...], kown[...])
    obv[...] = place(vg[...], vsum_own[...])
    out_k = remote(obk.at[other], ko_ref.at[:, my_cols], O_K, 0, 0, at_core())
    out_v = remote(obv.at[other], vo_ref.at[:, my_cols], O_V, 0, 0, at_core())
    out_k.start()
    out_v.start()
    keep_k = pltpu.make_async_copy(obk.at[c], ko_ref.at[:, my_cols], lsem.at[7])
    keep_v = pltpu.make_async_copy(obv.at[c], vo_ref.at[:, my_cols], lsem.at[8])
    keep_k.start()
    keep_v.start()

    def from_y(n):
        i = nth(n)
        remote(here, piece(dp, i), GY, i, i, at_y(i)).wait_recv()
        to_x(n)

    span(1, NY, from_y)

    def pass_on(n):
        ref = piece(x_up, nth(n))
        arrived(ref, GX, FROM_RIGHT + n)
        pltpu.make_async_remote_copy(
            src_ref=ref, dst_ref=ref, send_sem=ssem.at[SENDS[GR]], recv_sem=rsem.at[ARRIVALS[GX] + FROM_ACROSS],
            device_id=at_x(x_dn), device_id_type=MESH,
        ).start()

    span(0, 4, pass_on)
    keep(dp).start()

    left(krow.at[pl.ds(0, 112)], RKZ)
    span(0, y, lambda i: remote(vrow.at[i], vry.at[y], RVY, i, y, at_y(i)).wait_send())
    left(wzr.at[pl.ds(0, NZ - 1)], WZ)

    def from_x(i, first, at):
        arrived(wo_ref.at[wrows(i), pl.ds(0, (NY - first) * 128)], GX, at)
        remote(wo_ref.at[wrows(i)], out_rows(c, i), GD, 0, 0, at_core()).start()
        keep(i).start()

    from_x(x_up, 4, FROM_RIGHT + 4)
    from_x(x_dn, 0, FROM_LEFT)
    from_x(across, 0, FROM_ACROSS)
    arrived(out_rows(other, dp), GC)
    arrived(wout_ref.at[pl.ds(0, 192)], GD)
    pltpu.make_async_copy(wo_ref, wout_ref.at[pl.ds(0, HALF)], lsem.at[9]).wait()
    keep_q.wait()
    keep_k.wait()
    keep_v.wait()

    out_q.wait()
    out_k.wait()
    out_v.wait()
    left(wo_ref.at[pl.ds(0, 64), pl.ds(0, 896)], GY)
    left(mine, GC)
    left(mine, GX, x_up)
    left(mine, GX, x_dn)
    left(wo_ref.at[wrows(dp), pl.ds(0, D // 2)], GX, across)
    left(wo_ref.at[pl.ds(0, 64), pl.ds(0, D // 2)], GR)
    left(wo_ref.at[pl.ds(0, 192)], GD)


def store(*refs):
    arrays, outs, held, sem = refs[:4], refs[4:8], refs[8:12], refs[12]
    parts = [(3, 128 * i) for i in range(4)] + [(0, 0), (1, 0), (2, 0)]

    def moves(source, target, row):
        return [
            pltpu.make_async_copy(source[a].at[pl.ds(r, SEG)], target[a].at[pl.ds(r, SEG)], sem.at[row, i])
            for i, (a, r) in enumerate(parts)
        ]

    loads, stores = moves(arrays, held, 0), moves(held, outs, 1)
    for copy in loads:
        copy.start()
    for load, copy in zip(loads, stores):
        load.wait()
        copy.start()
    for copy in stores:
        copy.wait()


def on_device(query_rows, key_rows, value_rows, out_grad, out_weight, memory_index):
    V = pltpu.VMEM
    scratch = [
        pltpu.SMEM((MEM,), jnp.int32), V((2, MEM, SEG), jnp.int32),
        V((2, SEG, HALF), BF16), V((2, SEG, HALF), BF16), V((2, SEG, HALF), BF16),
        V((2, SEG, D), BF16), V((HALF, D), BF16),
        V((COLS, HALF), BF16), V((COLS, HALF), BF16), V((HALF, HALF), F32),
        V((16, HALF), BF16),
        V((NY, SEG, HALF), BF16), V((NY, SEG, HALF), BF16),
        V((NY, SEG, COLS), F32), V((2 * SEG, COLS), F32),
        V((8, COLS), F32), V((8, COLS), F32),
        V((HALF, HALF), F32), V((HALF, HALF), F32),
        V((NY, SEG, HALF), BF16), V((NY, SEG, HALF), BF16),
        V((HALF, HALF), F32), V((HALF, HALF), F32),
        V((NY, SEG, HALF), BF16), V((NZ, 16, HALF), BF16),
        V((NZ, NY, 16, HALF), BF16), V((NY, 16, HALF), BF16),
        V((SEG, HALF), F32), V((NY, 16, HALF), F32), V((16, HALF), F32),
        V((SEG, HALF), BF16), V((NY, 16, HALF), BF16),
        V((HALF, D), F32), V((HALF, D), BF16),
        V((NX, 64, D), BF16), V((64, D), BF16),
        V((NY, 64, 128), BF16), V((64, 128), F32),
        V((NZ, 64, 128), BF16), V((HALF, D), BF16),
        V((2, SEG, HALF), BF16), V((2, SEG, HALF), BF16), V((2, SEG, HALF), BF16),
        pltpu.SemaphoreType.DMA((SENDS[-1],)), pltpu.SemaphoreType.DMA((ARRIVALS[-1],)), pltpu.SemaphoreType.DMA((10,)),
    ]
    qg, kgrad, vgrad, wgrad = pl.pallas_call(
        kernel,
        out_shape=(
            jax.ShapeDtypeStruct((SEG, HD), BF16),
            jax.ShapeDtypeStruct((SEG, HD), BF16),
            jax.ShapeDtypeStruct((SEG, HD), BF16),
            jax.ShapeDtypeStruct((HD, D), BF16),
        ),
        in_specs=[pl.BlockSpec(memory_space=pltpu.HBM)] * 6,
        out_specs=[pl.BlockSpec(memory_space=pltpu.HBM)] * 4,
        scratch_shapes=scratch,
        compiler_params=pltpu.CompilerParams(
            collective_id=0, has_side_effects=True, vmem_limit_bytes=64 * 2**20
        ),
        name="memory_attention_backward",
    )(memory_index[0], query_rows[0], key_rows[0], value_rows[0], out_grad[0], out_weight)
    qg, kgrad, vgrad, wgrad = pl.pallas_call(
        store,
        out_shape=tuple(jax.ShapeDtypeStruct(a.shape, a.dtype) for a in (qg, kgrad, vgrad, wgrad)),
        in_specs=[pl.BlockSpec(memory_space=pltpu.HBM)] * 4,
        compiler_params=pltpu.CompilerParams(vmem_limit_bytes=64 * 2**20),
        out_specs=[pl.BlockSpec(memory_space=pltpu.HBM)] * 4,
        scratch_shapes=[V((SEG, HD), BF16)] * 3 + [V((HD, D), BF16), pltpu.SemaphoreType.DMA((2, 7))],
        name="store_results",
    )(qg, kgrad, vgrad, wgrad)
    return qg[None], kgrad[None], vgrad[None], wgrad


def solution(mesh):
    placed = (
        P("dp", "tm", None),
        P("dp", "tm", None),
        P("dp", "tm", None),
        P("dp", "tm", None),
        P(),
        P("dp", "tm", None),
    )
    return jax.shard_map(
        on_device,
        mesh=mesh,
        in_specs=placed,
        out_specs=(P("dp", "tm", None), P("dp", "tm", None), P("dp", "tm", None), P()),
        check_vma=False,
    )
```

```python
import math

import jax
import jax.numpy as jnp
from jax import lax
from jax.experimental import pallas as pl
from jax.experimental.pallas import tpu as pltpu
from jax.sharding import PartitionSpec as P

HEAD_DIM = 64
SEG = 128
MEM = 8
HD = 512
D = 1024
HALF = 256
HEADS = 4
COLS = HEADS * 2 * SEG
NY, NZ, NX = 8, 8, 4
MESH = pl.DeviceIdType.MESH
F32, BF16 = jnp.float32, jnp.bfloat16

PARTS = 2
(
    C_IDX, C_K, C_V, C_Q, C_G, KZ, KU, KD, VY, VU, VD, RKY, RKZ, RVZ, RVZ1, RVY,
    WX, WY, WZ, GY, GX, GR, GC, GD, O_Q, O_K, O_V,
) = range(27)
COUNTS = [(1, 1)] * 27
COUNTS[KU], COUNTS[KD], COUNTS[VU], COUNTS[VD] = (4 * PARTS,) * 2, (3 * PARTS,) * 2, (1, 4 * PARTS), (1, 3 * PARTS)
COUNTS[VY] = COUNTS[RKY] = (NY, NY)
COUNTS[RVY] = (0, 0)
COUNTS[GY], COUNTS[GX] = (1, NY), (NX, 7)
SENDS = [sum(n for n, _ in COUNTS[:i]) for i in range(28)]
ARRIVALS = [sum(n for _, n in COUNTS[:i]) for i in range(28)]
SENDS[RVY], ARRIVALS[RVY] = SENDS[VY], ARRIVALS[VY]
FROM_RIGHT, FROM_LEFT, FROM_ACROSS = 0, 5, 6


def nt(a, b):
    return lax.dot_general(a, b, (((1,), (1,)), ((), ())), preferred_element_type=F32)


def tn(a, b):
    return lax.dot_general(a, b, (((0,), (0,)), ((), ())), preferred_element_type=F32)


def nn(a, b):
    return jnp.dot(a, b, preferred_element_type=F32)


def rows8(block, op):
    return op(block.reshape(block.shape[0] // 8, 8, block.shape[1]), axis=0)


def kernel(
    idx_in, q_ref, k_ref, v_ref, g_ref, w_ref,
    qo_ref, ko_ref, vo_ref, wout_ref,
    idx_ref, idxb, kp, vp, qp, gp, wh, q4, ga4, gat, oh, kbuf, vbuf, s_mem, s_loc,
    m8, l8, acc, qacc, kt, vt, kg, vg, kry, krz, vrz, vry, ksum, vsum, vsum_own, krow, vrow,
    wt, wsend, wxr, wxs, wyr, wys, wzr, wo_ref, obq, obk, obv,
    ssem, rsem, lsem,
):
    dp, tm = lax.axis_index("dp"), lax.axis_index("tm")
    c, z, y = tm % 2, (tm // 2) % NZ, tm // (2 * NZ)
    other = 1 - c

    def at_core():
        return (dp, y * 16 + z * 2 + other)

    def at_z(i):
        return (dp, y * 16 + i * 2 + c)

    def at_y(i):
        return (dp, i * 16 + z * 2 + c)

    def at_x(i):
        return (i, tm)

    def remote(src, dst, phase, mine, theirs, device):
        return pltpu.make_async_remote_copy(
            src_ref=src, dst_ref=dst, send_sem=ssem.at[SENDS[phase] + mine],
            recv_sem=rsem.at[ARRIVALS[phase] + theirs],
            device_id=device, device_id_type=MESH,
        )

    def far(count, k):
        return count // 2 + (1 - 2 * (k % 2)) * ((k + 1) // 2)

    def arrived(ref, phase, at=0):
        remote(ref, ref, phase, 0, at, at_core()).wait_recv()

    def left(ref, phase, at=0):
        remote(ref, ref, phase, at, 0, at_core()).wait_send()

    def each(count, me, body, near=False):
        def step(k, _):
            body((me + far(count, count - 2 - k if near else k)) % count)
            return 0

        lax.fori_loop(0, count - 1, step, 0)

    def span(lo, hi, body):
        def step(i, _):
            body(i)
            return 0

        lax.fori_loop(lo, hi, step, 0)

    def blk(i):
        return pl.ds(pl.multiple_of(i * 16, 16), 16)

    my_cols = pl.ds(pl.multiple_of(c * HALF, HALF), HALF)
    their_cols = pl.ds(pl.multiple_of(other * HALF, HALF), HALF)

    kbuf[...] = jnp.zeros_like(kbuf)
    vbuf[...] = jnp.zeros_like(vbuf)

    bar = pltpu.get_barrier_semaphore()

    def greet(device):
        pl.semaphore_signal(bar, inc=1, device_id=device, device_id_type=MESH)

    greet(at_core())
    each(NZ, z, lambda i: greet(at_z(i)))
    each(NY, y, lambda i: greet(at_y(i)))
    each(NX, dp, lambda i: greet(at_x(i)))

    local = [
        pltpu.make_async_copy(src, dst, lsem.at[i])
        for i, (src, dst) in enumerate((
            (idx_in.at[0], idx_ref),
            (k_ref.at[:, my_cols], kp.at[c]),
            (v_ref.at[:, my_cols], vp.at[c]),
            (q_ref.at[:, my_cols], qp.at[c]),
            (g_ref, gp.at[c]),
            (w_ref.at[pl.ds(pl.multiple_of(c * HALF, HALF), HALF)], wh),
        ))
    ]
    for copy in local:
        copy.start()

    vt[...] = jnp.zeros_like(vt)
    pl.semaphore_wait(bar, 1 + (NZ - 1) + (NY - 1) + (NX - 1))

    swaps = [
        remote(idxb.at[c], idxb.at[c], C_IDX, 0, 0, at_core()),
        remote(k_ref.at[:, their_cols], kp.at[c], C_K, 0, 0, at_core()),
        remote(v_ref.at[:, their_cols], vp.at[c], C_V, 0, 0, at_core()),
        remote(q_ref.at[:, their_cols], qp.at[c], C_Q, 0, 0, at_core()),
        remote(g_ref, gp.at[c], C_G, 0, 0, at_core()),
    ]
    swaps[1].start()
    swaps[2].start()
    local[0].wait()
    sub = lax.broadcasted_iota(jnp.int32, (MEM, SEG), 0)
    idx = jnp.zeros((MEM, SEG), jnp.int32)
    for m in range(MEM):
        idx = jnp.where(sub == m, idx_ref[m], idx)
    idxb[c] = idx
    swaps[0].start()
    swaps[3].start()
    swaps[4].start()
    local[1].wait()
    for s in swaps[:2]:
        s.wait_recv()

    lane = lax.broadcasted_iota(jnp.int32, (MEM, SEG), 1)
    zero = jnp.zeros((MEM, SEG), F32)
    one_a = jnp.where(idxb[0] == lane, 1.0, 0.0).astype(F32)
    one_b = jnp.where(idxb[1] == lane, 1.0, 0.0).astype(F32)
    oh[...] = jnp.concatenate(
        [jnp.concatenate([one_a, zero], 1), jnp.concatenate([zero, one_b], 1)], 0
    ).astype(BF16)
    k_pair = kp[...].reshape(2 * SEG, HALF)
    kbuf[y, blk(z)] = nn(oh[...], k_pair).astype(BF16)

    each(NZ, z, lambda i: remote(kbuf.at[y, blk(z)], kbuf.at[y, blk(z)], KZ, 0, 0, at_z(i)).start())
    local[2].wait()
    swaps[2].wait_recv()
    v_pair = vp[...].reshape(2 * SEG, HALF)
    vbuf[y, blk(z)] = nn(oh[...], v_pair).astype(BF16)
    span(0, NY - 1 - y, lambda i: remote(vbuf.at[y, blk(z)], vbuf.at[y, blk(z)], VY, NY - 1 - i, y, at_y(NY - 1 - i)).start())

    local[3].wait()
    swaps[3].wait_recv()
    lanes = lax.broadcasted_iota(jnp.int32, (2 * SEG, HALF), 1) // HEAD_DIM
    q_pair = (qp[...].reshape(2 * SEG, HALF).astype(F32) * (1.0 / math.sqrt(HEAD_DIM))).astype(BF16)
    for h in range(HEADS):
        q4[pl.ds(h * 256, 256), :] = jnp.where(lanes == h, q_pair, jnp.zeros_like(q_pair))

    def score_block(keys):
        return nt(keys, q4[...])

    col = lax.broadcasted_iota(jnp.int32, (2 * SEG, COLS), 1)
    row = lax.broadcasted_iota(jnp.int32, (2 * SEG, COLS), 0)
    s = score_block(k_pair)
    s = jnp.where((row // SEG) == ((col // SEG) % 2), s, -jnp.inf)
    s_loc[...] = s
    m8[...] = rows8(s, jnp.max)

    local[4].wait()
    local[5].wait()
    swaps[4].wait_recv()
    g_pair = gp[...].reshape(2 * SEG, D)
    ga = nt(g_pair, wh[...]).astype(BF16)
    gat[...] = nt(wh[...], g_pair).astype(BF16).astype(F32)
    for h in range(HEADS):
        ga4[pl.ds(h * 256, 256), :] = jnp.where(lanes == h, ga, jnp.zeros_like(ga))

    arrived(kbuf.at[y, pl.ds(0, 112)], KZ)

    up_y, dn_y, up_z, dn_z = (y + 1) % NY, (y + NY - 1) % NY, (z + 1) % NZ, (z + NZ - 1) % NZ

    def k_pass(phase, device, b, part, hops):
        ref = kbuf.at[b, pl.ds(part * (SEG // PARTS), SEG // PARTS)]
        at = hops * PARTS + part
        return remote(ref, ref, phase, at, at, device)

    def v_pass(phase, device, b, part, hops):
        ref = vbuf.at[pl.ds(part * (NY // PARTS), NY // PARTS), blk(b)]
        return remote(ref, ref, phase, 0, hops * PARTS + part, device)

    def k_up(b, part, hops):
        return k_pass(KU, at_y(up_y), b, part, hops)

    def k_dn(b, part, hops):
        return k_pass(KD, at_y(dn_y), b, part, hops)

    def v_up(b, part, hops):
        return v_pass(VU, at_z(up_z), b, part, hops)

    def v_dn(b, part, hops):
        return v_pass(VD, at_z(dn_z), b, part, hops)

    def begin(copy, b):
        for part in range(PARTS):
            copy(b, part, 0).start()

    def hand_on(copy, b, step, more):
        for part in range(PARTS):
            copy(b, part, step - 1).wait_recv()

            @pl.when(more)
            def _():
                copy(b, part, step).start()

    @pl.when(y < NY - 1)
    def _():
        begin(k_up, y)

    @pl.when(y <= 2)
    def _():
        begin(k_dn, y)

    span(0, y, lambda i: remote(vbuf.at[y, blk(z)], vbuf.at[i, blk(z)], VY, i, i, at_y(i)).wait_recv())
    begin(v_up, z)
    begin(v_dn, z)

    def masked(block):
        at = lax.broadcasted_iota(jnp.int32, (SEG, COLS), 0) // MEM
        seg = 2 * z + (lax.broadcasted_iota(jnp.int32, (SEG, COLS), 1) // SEG) % 2
        return jnp.where(at < seg, block, -jnp.inf)

    s = masked(score_block(kbuf[y]))
    s_mem[y] = s
    m8[...] = jnp.maximum(m8[...], rows8(s, jnp.max))

    def scores_of(i):
        block = score_block(kbuf[i])
        s_mem[i] = block
        m8[...] = jnp.maximum(m8[...], rows8(block, jnp.max))

    def gather_step(step):
        below, above = y - step, (y + step) % NY
        from_above = (step <= 3) & (above <= 2)

        @pl.when(below >= 0)
        def _():
            hand_on(k_up, below, step, (step < 4) & (y < NY - 1))

        @pl.when(from_above)
        def _():
            hand_on(k_dn, above, step, step < 3)

        @pl.when(step <= 3)
        def _():
            hand_on(v_up, (z + NZ - step) % NZ, step, step < 4)
            hand_on(v_dn, (z + step) % NZ, step, step < 3)

        @pl.when(below >= 0)
        def _():
            scores_of(below)

        @pl.when(from_above & (above < y))
        def _():
            scores_of(above)

    span(1, 5, gather_step)
    pairs = y // 2 + 1

    @pl.when(y % 2 == 0)
    def _():
        s_mem[y + 1] = jnp.full((SEG, COLS), -jnp.inf, F32)

    def two(i):
        return pl.ds(2 * i, 2)

    top = jnp.max(m8[...], axis=0, keepdims=True)

    def add_attended(values, p):
        p_low = p.astype(BF16)
        vals_t = values.T
        for h in range(HEADS):
            rows = pl.ds(h * HEAD_DIM, HEAD_DIM)
            acc[rows, :] = acc[rows, :] + nn(
                vals_t[h * HEAD_DIM : (h + 1) * HEAD_DIM], p_low[:, h * 256 : (h + 1) * 256]
            )

    p = jnp.exp(s_loc[...] - top)
    s_loc[...] = p
    l8[...] = rows8(p, jnp.sum)
    acc[...] = jnp.zeros_like(acc)
    add_attended(v_pair, p)

    def soft_of(i):
        p = jnp.exp(s_mem[two(i)].reshape(2 * SEG, COLS) - top)
        s_mem[two(i)] = p.reshape(2, SEG, COLS)
        l8[...] = l8[...] + rows8(p, jnp.sum)

    span(0, pairs, soft_of)

    for part in range(PARTS):
        v_up((z + NZ - 4) % NZ, part, 3).wait_recv()

    def attended_of(i):
        add_attended(vbuf[two(i)].reshape(2 * SEG, HALF), s_mem[two(i)].reshape(2 * SEG, COLS))

    span(0, pairs, attended_of)
    inv = 1.0 / jnp.sum(l8[...], axis=0, keepdims=True)
    att = jnp.concatenate(
        [acc[h * HEAD_DIM : (h + 1) * HEAD_DIM, :] * inv[:, h * 256 : (h + 1) * 256] for h in range(HEADS)], 0
    ).astype(BF16)
    term = nn(att, g_pair)
    wt[...] = term
    wsend[...] = term.astype(BF16)

    def wrows(i):
        return pl.ds(pl.multiple_of(i * 64, 64), 64)

    each(NX, dp, lambda i: remote(wsend.at[wrows(i)], wxr.at[dp], WX, 0, 0, at_x(i)).start())

    prod = att.astype(F32) * gat[...]
    delta = jnp.concatenate(
        [jnp.sum(prod[h * HEAD_DIM : (h + 1) * HEAD_DIM, :], axis=0, keepdims=True) for h in range(HEADS)], 1
    )

    def back(keys, values, p):
        pn = p * inv
        soft = nt(values, ga4[...])
        gs = (pn * (soft - delta)).astype(BF16)
        k_term = nn(gs, q4[...])
        v_term = nn(pn.astype(BF16), ga4[...])
        keys_t = keys.T
        for h in range(HEADS):
            rows = pl.ds(h * HEAD_DIM, HEAD_DIM)
            qacc[rows, :] = qacc[rows, :] + nn(
                keys_t[h * HEAD_DIM : (h + 1) * HEAD_DIM], gs[:, h * 256 : (h + 1) * 256]
            )
        return k_term, v_term

    qacc[...] = jnp.zeros_like(qacc)

    def back_of(i):
        k_term, v_term = back(
            kbuf[two(i)].reshape(2 * SEG, HALF), vbuf[two(i)].reshape(2 * SEG, HALF),
            s_mem[two(i)].reshape(2 * SEG, COLS),
        )
        kt[two(i)] = k_term.astype(BF16).reshape(2, SEG, HALF)
        vt[two(i)] = v_term.astype(BF16).reshape(2, SEG, HALF)
        for j in (2 * i, 2 * i + 1):
            @pl.when(j < y)
            def _():
                remote(kt.at[j], kry.at[y], RKY, j, y, at_y(j)).start()

        @pl.when(i == 1)
        def _():
            v_half(0)

    def v_send(half, i):
        part = pl.ds(half * 4, 4)
        return remote(vt.at[part, blk(i)], vrz.at[z, part], RVZ + half, 0, 0, at_z(i))

    def v_half(half):
        each(NZ, z, lambda i: v_send(half, i).start())

    span(0, pairs, back_of)

    @pl.when(y < 2)
    def _():
        v_half(0)

    @pl.when(y >= 4)
    def _():
        v_half(1)

    k_term, v_term = back(k_pair, v_pair, s_loc[...])
    kg[...] = k_term
    vg[...] = v_term
    qg = (qacc[...] * (1.0 / math.sqrt(HEAD_DIM))).T.astype(BF16)
    obq[...] = qg.reshape(2, SEG, HALF)
    out_q = remote(obq.at[other], qo_ref.at[:, my_cols], O_Q, 0, 0, at_core())
    out_q.start()
    keep_q = pltpu.make_async_copy(obq.at[c], qo_ref.at[:, my_cols], lsem.at[6])
    keep_q.start()

    for s in swaps:
        s.wait_send()
    left(kbuf.at[y, pl.ds(0, 112)], KZ)
    span(y + 1, NY, lambda i: remote(vbuf.at[y, blk(z)], vbuf.at[y, blk(z)], VY, i, y, at_y(i)).wait_send())

    def sent(copy, b, step):
        for part in range(PARTS):
            copy(b, part, step).wait_send()

    def gather_sent(step):
        below, above = y - step, (y + step) % NY

        @pl.when((below >= 0) & (y < NY - 1))
        def _():
            sent(k_up, below, step)

        @pl.when((step < 3) & (above <= 2))
        def _():
            sent(k_dn, above, step)

    span(0, 4, gather_sent)
    left(vbuf.at[:, pl.ds(0, 64)], VU)
    left(vbuf.at[:, pl.ds(0, 48)], VD)

    arrived(wxr.at[pl.ds(0, NX - 1)], WX)

    def add_x(i):
        wt[wrows(dp), :] = wt[wrows(dp), :] + wxr[i].astype(F32)

    each(NX, dp, add_x, near=True)
    wxs[...] = wt[wrows(dp), :].astype(BF16)

    def wcols(i):
        return pl.ds(pl.multiple_of(i * 128, 128), 128)

    each(NY, y, lambda i: remote(wxs.at[:, wcols(i)], wyr.at[y], WY, 0, 0, at_y(i)).start())
    left(wsend.at[pl.ds(0, 192)], WX)

    wys[...] = wt[wrows(dp), wcols(y)]

    arrived(wyr.at[pl.ds(0, NY - 1)], WY)

    def add_y(i):
        wys[...] = wys[...] + wyr[i].astype(F32)

    each(NY, y, add_y, near=True)
    wzr[z] = wys[...].astype(BF16)
    each(NZ, z, lambda i: remote(wzr.at[z], wzr.at[z], WZ, 0, 0, at_z(i)).start())
    left(wxs.at[:, pl.ds(0, 896)], WY)
    span(0, y, lambda i: remote(kt.at[i], kry.at[y], RKY, i, y, at_y(i)).wait_send())

    ksum[...] = kt[y].astype(F32)

    def add_ky(i):
        remote(kt.at[0], kry.at[i], RKY, 0, i, at_y(i)).wait_recv()
        ksum[...] = ksum[...] + kry[i].astype(F32)

    span(y + 1, NY, add_ky)
    krow[...] = ksum[...].astype(BF16)
    each(NZ, z, lambda i: remote(krow.at[blk(i)], krz.at[z], RKZ, 0, 0, at_z(i)).start())

    def add_vz(half):
        part = pl.ds(half * 4, 4)
        arrived(vrz.at[pl.ds(0, NZ - 1), part], RVZ + half)
        left(vt.at[part, pl.ds(0, 112)], RVZ + half)
        vsum[part] = vt[part, blk(z)].astype(F32)

        def add(i):
            vsum[part] = vsum[part] + vrz[i, part].astype(F32)

        each(NZ, z, add, near=True)

    add_vz(0)

    @pl.when(y >= 4)
    def _():
        add_vz(1)

    vrow[...] = vsum[...].astype(BF16)
    span(0, y, lambda i: remote(vrow.at[i], vry.at[y], RVY, i, y, at_y(i)).start())

    arrived(wzr.at[pl.ds(0, NZ - 1)], WZ)
    total = wzr[0].astype(F32)
    for i in range(1, NZ):
        total = total + wzr[i].astype(F32)

    def piece(i, j):
        return wo_ref.at[wrows(i), wcols(j)]

    def out_rows(half, i):
        return wout_ref.at[pl.ds(pl.multiple_of(half * HALF + i * 64, 64), 64)]

    def out_piece(half, i, j):
        return wout_ref.at[pl.ds(pl.multiple_of(half * HALF + i * 64, 64), 64), wcols(j)]

    wo_ref[wrows(dp), wcols(y)] = (total * (1.0 / math.sqrt(4 * 16384))).astype(BF16)
    here = piece(dp, y)

    def send_x(i, j, at):
        return remote(piece(dp, j), piece(dp, j), GX, i, at, at_x(i))

    x_up, x_dn, across = (dp + 1) % NX, (dp + 3) % NX, (dp + 2) % NX

    def nth(n):
        return (y + (1 - 2 * (n % 2)) * ((n + 1) // 2)) % NY

    def to_x(n):
        j = nth(n)
        send_x(x_up, j, FROM_LEFT).start()
        send_x(x_dn, j, FROM_RIGHT + n - n // 4 * (n - 4)).start()

        @pl.when(n >= 4)
        def _():
            send_x(across, j, FROM_ACROSS).start()

        remote(piece(dp, j), out_piece(c, dp, j), GC, 0, 0, at_core()).start()

    mine = wo_ref.at[wrows(dp)]

    def keep(i):
        return pltpu.make_async_copy(wo_ref.at[wrows(i)], out_rows(c, i), lsem.at[9])

    each(NY, y, lambda i: remote(here, here, GY, 0, y, at_y(i)).start())
    to_x(0)

    vsum_own[...] = vsum[y]

    def add_vy(i):
        remote(vrow.at[0], vry.at[i], RVY, 0, i, at_y(i)).wait_recv()
        vsum_own[...] = vsum_own[...] + vry[i].astype(F32)

    span(y + 1, NY, add_vy)
    kown = ksum.at[blk(z)]

    arrived(krz.at[pl.ds(0, NZ - 1)], RKZ)

    def add_kz(i):
        kown[...] = kown[...] + krz[i].astype(F32)

    each(NZ, z, add_kz, near=True)

    def place(local, terms):
        hi = terms.astype(BF16)
        lo = (terms - hi.astype(F32)).astype(BF16)
        return (local + (tn(oh[...], hi) + tn(oh[...], lo))).astype(BF16).reshape(2, SEG, HALF)

    obk[...] = place(kg[...], kown[...])
    obv[...] = place(vg[...], vsum_own[...])
    out_k = remote(obk.at[other], ko_ref.at[:, my_cols], O_K, 0, 0, at_core())
    out_v = remote(obv.at[other], vo_ref.at[:, my_cols], O_V, 0, 0, at_core())
    out_k.start()
    out_v.start()
    keep_k = pltpu.make_async_copy(obk.at[c], ko_ref.at[:, my_cols], lsem.at[7])
    keep_v = pltpu.make_async_copy(obv.at[c], vo_ref.at[:, my_cols], lsem.at[8])
    keep_k.start()
    keep_v.start()

    def from_y(n):
        i = nth(n)
        remote(here, piece(dp, i), GY, i, i, at_y(i)).wait_recv()
        to_x(n)

    span(1, NY, from_y)

    def pass_on(n):
        ref = piece(x_up, nth(n))
        arrived(ref, GX, FROM_RIGHT + n)
        pltpu.make_async_remote_copy(
            src_ref=ref, dst_ref=ref, send_sem=ssem.at[SENDS[GR]], recv_sem=rsem.at[ARRIVALS[GX] + FROM_ACROSS],
            device_id=at_x(x_dn), device_id_type=MESH,
        ).start()

    span(0, 4, pass_on)
    keep(dp).start()

    left(krow.at[pl.ds(0, 112)], RKZ)
    span(0, y, lambda i: remote(vrow.at[i], vry.at[y], RVY, i, y, at_y(i)).wait_send())
    left(wzr.at[pl.ds(0, NZ - 1)], WZ)

    def from_x(i, first, at):
        arrived(wo_ref.at[wrows(i), pl.ds(0, (NY - first) * 128)], GX, at)
        remote(wo_ref.at[wrows(i)], out_rows(c, i), GD, 0, 0, at_core()).start()
        keep(i).start()

    from_x(x_up, 4, FROM_RIGHT + 4)
    from_x(x_dn, 0, FROM_LEFT)
    from_x(across, 0, FROM_ACROSS)
    arrived(out_rows(other, dp), GC)
    arrived(wout_ref.at[pl.ds(0, 192)], GD)
    pltpu.make_async_copy(wo_ref, wout_ref.at[pl.ds(0, HALF)], lsem.at[9]).wait()
    keep_q.wait()
    keep_k.wait()
    keep_v.wait()

    out_q.wait()
    out_k.wait()
    out_v.wait()
    left(wo_ref.at[pl.ds(0, 64), pl.ds(0, 896)], GY)
    left(mine, GC)
    left(mine, GX, x_up)
    left(mine, GX, x_dn)
    left(wo_ref.at[wrows(dp), pl.ds(0, D // 2)], GX, across)
    left(wo_ref.at[pl.ds(0, 64), pl.ds(0, D // 2)], GR)
    left(wo_ref.at[pl.ds(0, 192)], GD)


def store(*refs):
    arrays, outs, held, sem = refs[:4], refs[4:8], refs[8:12], refs[12]
    parts = [(3, 128 * i) for i in range(4)] + [(0, 0), (1, 0), (2, 0)]

    def moves(source, target, row):
        return [
            pltpu.make_async_copy(source[a].at[pl.ds(r, SEG)], target[a].at[pl.ds(r, SEG)], sem.at[row, i])
            for i, (a, r) in enumerate(parts)
        ]

    loads, stores = moves(arrays, held, 0), moves(held, outs, 1)
    for copy in loads:
        copy.start()
    for load, copy in zip(loads, stores):
        load.wait()
        copy.start()
    for copy in stores:
        copy.wait()


def on_device(query_rows, key_rows, value_rows, out_grad, out_weight, memory_index):
    V = pltpu.VMEM
    scratch = [
        pltpu.SMEM((MEM,), jnp.int32), V((2, MEM, SEG), jnp.int32),
        V((2, SEG, HALF), BF16), V((2, SEG, HALF), BF16), V((2, SEG, HALF), BF16),
        V((2, SEG, D), BF16), V((HALF, D), BF16),
        V((COLS, HALF), BF16), V((COLS, HALF), BF16), V((HALF, HALF), F32),
        V((16, HALF), BF16),
        V((NY, SEG, HALF), BF16), V((NY, SEG, HALF), BF16),
        V((NY, SEG, COLS), F32), V((2 * SEG, COLS), F32),
        V((8, COLS), F32), V((8, COLS), F32),
        V((HALF, HALF), F32), V((HALF, HALF), F32),
        V((NY, SEG, HALF), BF16), V((NY, SEG, HALF), BF16),
        V((HALF, HALF), F32), V((HALF, HALF), F32),
        V((NY, SEG, HALF), BF16), V((NZ, 16, HALF), BF16),
        V((NZ, NY, 16, HALF), BF16), V((NY, 16, HALF), BF16),
        V((SEG, HALF), F32), V((NY, 16, HALF), F32), V((16, HALF), F32),
        V((SEG, HALF), BF16), V((NY, 16, HALF), BF16),
        V((HALF, D), F32), V((HALF, D), BF16),
        V((NX, 64, D), BF16), V((64, D), BF16),
        V((NY, 64, 128), BF16), V((64, 128), F32),
        V((NZ, 64, 128), BF16), V((HALF, D), BF16),
        V((2, SEG, HALF), BF16), V((2, SEG, HALF), BF16), V((2, SEG, HALF), BF16),
        pltpu.SemaphoreType.DMA((SENDS[-1],)), pltpu.SemaphoreType.DMA((ARRIVALS[-1],)), pltpu.SemaphoreType.DMA((10,)),
    ]
    qg, kgrad, vgrad, wgrad = pl.pallas_call(
        kernel,
        out_shape=(
            jax.ShapeDtypeStruct((SEG, HD), BF16),
            jax.ShapeDtypeStruct((SEG, HD), BF16),
            jax.ShapeDtypeStruct((SEG, HD), BF16),
            jax.ShapeDtypeStruct((HD, D), BF16),
        ),
        in_specs=[pl.BlockSpec(memory_space=pltpu.HBM)] * 6,
        out_specs=[pl.BlockSpec(memory_space=pltpu.HBM)] * 4,
        scratch_shapes=scratch,
        compiler_params=pltpu.CompilerParams(
            collective_id=0, has_side_effects=True, vmem_limit_bytes=64 * 2**20
        ),
        name="memory_attention_backward",
    )(memory_index[0], query_rows[0], key_rows[0], value_rows[0], out_grad[0], out_weight)
    qg, kgrad, vgrad, wgrad = pl.pallas_call(
        store,
        out_shape=tuple(jax.ShapeDtypeStruct(a.shape, a.dtype) for a in (qg, kgrad, vgrad, wgrad)),
        in_specs=[pl.BlockSpec(memory_space=pltpu.HBM)] * 4,
        compiler_params=pltpu.CompilerParams(vmem_limit_bytes=64 * 2**20),
        out_specs=[pl.BlockSpec(memory_space=pltpu.HBM)] * 4,
        scratch_shapes=[V((SEG, HD), BF16)] * 3 + [V((HD, D), BF16), pltpu.SemaphoreType.DMA((2, 7))],
        name="store_results",
    )(qg, kgrad, vgrad, wgrad)
    return qg[None], kgrad[None], vgrad[None], wgrad


def solution(mesh):
    placed = (
        P("dp", "tm", None),
        P("dp", "tm", None),
        P("dp", "tm", None),
        P("dp", "tm", None),
        P(),
        P("dp", "tm", None),
    )
    return jax.shard_map(
        on_device,
        mesh=mesh,
        in_specs=placed,
        out_specs=(P("dp", "tm", None), P("dp", "tm", None), P("dp", "tm", None), P()),
        check_vma=False,
    )
```
